256 devices in a mesh: slab: 32 (over x, z), head: 8 (over y, core).
Axes of the slice: x: 4, y: 4, z: 8, core: 2. Of those that a mesh axis runs over, the one named last changes fastest.
Arguments:
- activations: bfloat16 [12288, 5120], P('slab', 'head'), may hold values from -16 to 16
- w_query: bfloat16 [5120, 3072], P('slab', 'head'), may hold values from -64 to 64
- w_key: bfloat16 [5120, 3072], P('slab', 'head'), may hold values from -64 to 64
- w_value: bfloat16 [5120, 3072], P('slab', 'head'), may hold values from -0.078125 to 0.078125
- query_gain: float32 [3072], P('head'), may hold values from 0.4 to 7.2
- key_gain: float32 [3072], P('head'), may hold values from 0.4 to 7.2
- w_output: bfloat16 [3072, 5120], P('head', 'slab'), may hold values from -0.109375 to 0.109375
- kv_tiles: int32 [32, 3], P('slab'), may hold values from 0 to 31, as said below
- kv_count: int32 [32], P('slab'), may hold values from 1 to 3, as said below
Outputs:
- attn_out: bfloat16 [12288, 5120], P('slab', 'head')
The draws below stay inside these ranges and needn't reach their ends.
Inputs may be any that keep to these rules, and one draw needn't show every extreme that they name: `kv_tiles`: tile t belongs to slab t. Row i lists tiles of tile i's slab and of the slabs just before and after it; its first kv_count[i] entries are distinct and the first is i itself; later entries are ignored. kv_count[i] is at most the number of tiles in tile i's slab and its neighbouring slabs.
All inputs are finite; a program needn't handle non-finite values.
Results may differ from the reference program's by a relative error of at most 0.019.
Values may be sent and summed in bfloat16 or wider, within the bound.
No kernel may reach another device: no remote copies, remote signals or barrier semaphores. Data moves between devices by JAX's collectives and lax.ppermute only.
A program may use at most 64 MiB of HBM per device.

```python
import math
import jax
import jax.numpy as jnp
from jax import lax

D = 5120
HD = 128
TILE = 384
TILES_DEV = 1
HEADS = 24
HD_ALL = 3072
TILES = 32
TOKENS = 12288
WINDOW = 3


def column_weights(key, rise):
    normal_part = jnp.clip(jax.random.normal(jax.random.fold_in(key, 7), (D, HD_ALL), jnp.float32), -5.0, 5.0)
    column_pos = jnp.arange(HD_ALL, dtype=jnp.float32) / (HD_ALL - 1)
    spread_part = jnp.exp(jax.random.uniform(jax.random.fold_in(key, 8), (HD_ALL,), jnp.float32, 0.0, math.log(10.0)))
    return normal_part * D ** (-0.5) * jnp.exp(math.log(rise) * column_pos)[None, :] * spread_part[None, :]


def tile_lists(key):
    tile_ids = jnp.arange(TILES, dtype=jnp.int32)
    slab_ids = tile_ids // TILES_DEV
    column_ids = jnp.arange(WINDOW, dtype=jnp.int32)[None, :]
    random_part = jax.random.randint(jax.random.fold_in(key, 11), (TILES, WINDOW), 0, 1 << 20, dtype=jnp.int32)
    shuffled = jnp.argsort(random_part * WINDOW + column_ids, axis=1).astype(jnp.int32)
    candidates = (slab_ids[:, None] - 1) * TILES_DEV + shuffled
    usable = (candidates >= 0) & (candidates < TILES)
    priority = jnp.where(candidates == tile_ids[:, None], -1, jnp.where(usable, column_ids, WINDOW + column_ids))
    placed = jnp.argsort(priority, axis=1).astype(jnp.int32)
    ordered = jnp.take_along_axis(candidates, placed, axis=1)
    usable_sorted = jnp.take_along_axis(usable, placed, axis=1)
    ordered = jnp.where(usable_sorted, ordered, tile_ids[:, None]).astype(jnp.int32)
    available = jnp.sum(usable.astype(jnp.int32), axis=1)
    dropped = jax.random.randint(jax.random.fold_in(key, 12), (TILES,), 0, available - TILES_DEV + 1, dtype=jnp.int32)
    counts = available - dropped
    chosen = jax.random.randint(jax.random.fold_in(key, 13), (), TILES_DEV, TILES - TILES_DEV, dtype=jnp.int32)
    counts = jnp.where(tile_ids == chosen, available, counts).astype(jnp.int32)
    return (ordered, counts)


def draw_activations(key, part):
    key = jax.random.fold_in(key, 1)
    first_key, second_key = jax.random.split(key)
    base_part = jnp.clip(jax.random.normal(first_key, (TOKENS, D), jnp.float32), -5.0, 5.0)
    row_scale = jnp.exp(jax.random.uniform(second_key, (TOKENS, 1), jnp.float32, math.log(0.3), math.log(3.0)))
    return (base_part * row_scale).astype(jnp.bfloat16)


def draw_w_query(key, part):
    shared = column_weights(key, 3.0)
    return shared.astype(jnp.bfloat16)


def draw_w_key(key, part):
    key = jax.random.fold_in(key, 2)
    result = column_weights(key, 3.0)
    return result.astype(jnp.bfloat16)


def gain_table(key):
    first_key = jax.random.fold_in(key, 0)
    return jax.random.uniform(first_key, (HD_ALL,), jnp.float32, 0.5, 1.5)


def draw_query_gain(key, part):
    key = jax.random.fold_in(key, 3)
    return gain_table(key)


def draw_key_gain(key, part):
    key = jax.random.fold_in(key, 4)
    return gain_table(key)


def draw_kv_tiles(key, part):
    return tile_lists(key)[0]


def draw_kv_count(key, part):
    return tile_lists(key)[1]


def block_scale(key, extent, cuts, least, largest):
    def one(dim, shards_of):
        heights = jax.random.uniform(jax.random.fold_in(jax.random.fold_in(key, 6), dim), (shards_of,), jnp.float32, least / len(cuts), largest / len(cuts))
        return jnp.repeat(jnp.exp(heights), extent[dim] // shards_of).reshape((-1,) + (1,) * (len(extent) - dim - 1))

    factor_of = one(*cuts[0])
    for cut in cuts[1:]:
        factor_of = factor_of * one(*cut)
    return factor_of


def centred(key, dims, width, bound, shards=(), kind=jnp.bfloat16):
    values = width * jax.random.normal(key, dims, jnp.float32)
    if shards:
        values = values * block_scale(key, dims, shards, -0.22, 0.18)
    return jnp.clip(values, -bound, bound).astype(kind)


def setup_inputs(seed: int = 0) -> dict:
    streams_of = jax.random.split(jax.random.key(seed), 10)
    return {
        "activations": draw_activations(jax.random.fold_in(streams_of[9], 71), 0),
        "w_query": draw_w_query(jax.random.fold_in(streams_of[9], 71), 0),
        "w_key": draw_w_key(jax.random.fold_in(streams_of[9], 71), 0),
        "w_value": centred(streams_of[3], (D, HD_ALL), D ** -0.5, 0.078125, ((0, 32), (1, 8))),
        "query_gain": draw_query_gain(jax.random.fold_in(streams_of[9], 71), 0),
        "key_gain": draw_key_gain(jax.random.fold_in(streams_of[9], 71), 0),
        "w_output": centred(streams_of[6], (HD_ALL, D), HD_ALL ** -0.5, 0.109375, ((0, 8), (1, 32))),
        "kv_tiles": draw_kv_tiles(jax.random.fold_in(streams_of[9], 71), 0),
        "kv_count": draw_kv_count(jax.random.fold_in(streams_of[9], 71), 0),
    }


norm_eps = 1e-06
masked_score = -1e+30

def normalize(raw, gain):
    mean_sq = lax.optimization_barrier(jnp.mean(raw * raw, axis=-1, keepdims=True))
    return (raw * lax.rsqrt(mean_sq + norm_eps) * gain).astype(jnp.bfloat16)

def reference(activations, w_query, w_key, w_value, query_gain, key_gain, w_output, kv_tiles, kv_count):
    q_raw = jnp.dot(activations, w_query, preferred_element_type=jnp.float32)
    k_raw = jnp.dot(activations, w_key, preferred_element_type=jnp.float32)
    value_tok = jnp.dot(activations, w_value, preferred_element_type=jnp.float32).astype(jnp.bfloat16)
    query_tok = normalize(q_raw, query_gain)
    key_tok = normalize(k_raw, key_gain)
    score_scale = HD ** (-0.5)
    query_all = query_tok.reshape(TILES, TILE, HEADS, HD)
    key_all = key_tok.reshape(TILES, TILE, HEADS, HD)
    value_all = value_tok.reshape(TILES, TILE, HEADS, HD)

    def attend_tile(operands):
        tile_list, live_count, query_tile = operands
        key_rows = key_all[tile_list].reshape(WINDOW * TILE, HEADS, HD)
        value_rows = value_all[tile_list].reshape(WINDOW * TILE, HEADS, HD)
        scores = jnp.einsum('qhd,khd->hqk', query_tile.astype(jnp.float32), key_rows.astype(jnp.float32)) * score_scale
        slot_live = jnp.repeat(jnp.arange(WINDOW, dtype=jnp.int32) < live_count, TILE)
        scores = jnp.where(slot_live[None, None, :], scores, masked_score)
        maxima = lax.optimization_barrier(jnp.max(scores, axis=2, keepdims=True))
        exp_scores = jnp.exp(scores - maxima)
        attn_probs = (exp_scores / lax.optimization_barrier(jnp.sum(exp_scores, axis=2, keepdims=True))).astype(jnp.bfloat16)
        attended = jnp.einsum('hqk,khd->qhd', attn_probs.astype(jnp.float32), value_rows.astype(jnp.float32))
        return attended.astype(jnp.bfloat16).reshape(TILE, HD_ALL)
    attended_all = lax.map(attend_tile, (kv_tiles, kv_count, query_all)).reshape(TOKENS, HD_ALL)
    return jnp.dot(attended_all, w_output, preferred_element_type=jnp.float32).astype(jnp.bfloat16)
```

```python
import jax
import jax.numpy as jnp
from jax import lax
from jax.experimental import pallas as pl
from jax.experimental.pallas import tpu as pltpu
from jax.sharding import PartitionSpec as P

HD = 128
NX, NZ, NY, NC = 4, 8, 4, 2

norm_eps = 1e-06
masked_score = -1e30
VMEM_LIMIT = 48 * 1024 * 1024
ANY = pl.BlockSpec(memory_space=pl.ANY)
SMEM = pl.BlockSpec(memory_space=pltpu.SMEM)
VMEM = pl.BlockSpec(memory_space=pltpu.VMEM)


def device(x, z, y, c):
    return ((x * NZ + z) * NY + y) * NC + c


def moved(cells, target):
    pairs = []
    for x in range(NX):
        for z in range(NZ):
            for y in range(NY):
                for c in range(NC):
                    pairs.append((device(x, z, y, c), device(*target(x, z, y, c))))
    return lax.ppermute(cells, ("slab", "head"), pairs)


def along_x(cells, step):
    return moved(cells, lambda x, z, y, c: ((x + step) % NX, z, y, c))


def along_z(cells, step):
    return moved(cells, lambda x, z, y, c: (x, (z + step) % NZ, y, c))


def along_y(cells, step):
    return moved(cells, lambda x, z, y, c: (x, z, (y + step) % NY, c))


def to_sibling(cells):
    return moved(cells, lambda x, z, y, c: (x, z, y, 1 - c))


def along_slab(cells, step):
    count = NX * NZ

    def target(x, z, y, c):
        slab = (x * NZ + z + step) % count
        return (slab // NZ, slab % NZ, y, c)

    return moved(cells, target)


def ring(cells, shift, count):
    pieces = [None] * count
    pieces[0] = cells
    ahead, behind = cells, cells
    for step in range(1, count // 2):
        ahead = shift(ahead, -1)
        behind = shift(behind, 1)
        pieces[step] = ahead
        pieces[count - step] = behind
    half = cells.shape[0] // 2
    pieces[count // 2] = (shift(ahead[:half], -1), shift(behind[half:], 1))
    return pieces


def place(pieces, first, width):
    count = len(pieces)
    cells = pieces[0]
    flat, where = [], []
    for d, piece in enumerate(pieces):
        if isinstance(piece, tuple):
            half = cells.shape[0] // 2
            flat += list(piece)
            where += [(d, 0, half), (d, half, half)]
        else:
            flat.append(piece)
            where.append((d, 0, cells.shape[0]))

    def kernel(first_ref, *refs):
        sources, out, sems = refs[: len(flat)], refs[-2], refs[-1]
        copies = []
        for i, (d, start, size) in enumerate(where):
            slot = lax.rem(first_ref[0] + d, count)
            copies.append(
                pltpu.make_async_copy(
                    sources[i], out.at[slot, pl.ds(start, size)], sems.at[i]
                )
            )
        for copy in copies:
            copy.start()
        for copy in copies:
            copy.wait()

    return pl.pallas_call(
        kernel,
        out_shape=jax.ShapeDtypeStruct((count,) + cells.shape, cells.dtype),
        in_specs=[SMEM] + [ANY] * len(flat),
        out_specs=ANY,
        scratch_shapes=[pltpu.SemaphoreType.DMA((len(flat),))],
        compiler_params=pltpu.CompilerParams(vmem_limit_bytes=VMEM_LIMIT),
    )(first.reshape(1), *flat)


def gather_zx(cells, x, z):
    own = place(ring(cells, along_z, NZ), z, NZ)
    chunks = []
    for d, piece in enumerate(ring(own, along_x, NX)):
        if isinstance(piece, tuple):
            chunks += [("x", d, 0, NZ // 2, piece[0]), ("x", d, NZ // 2, NZ // 2, piece[1])]
        else:
            chunks.append(("x", d, 0, NZ, piece))
    return chunks


def gather_xz(cells, x, z):
    own = place(ring(cells, along_x, NX), x, NX)
    chunks = []
    for d, piece in enumerate(ring(own, along_z, NZ)):
        if isinstance(piece, tuple):
            chunks += [("z", d, 0, NX // 2, piece[0]), ("z", d, NX // 2, NX // 2, piece[1])]
        else:
            chunks.append(("z", d, 0, NX, piece))
    return chunks


def weight_copies(chunks, refs, x, z, scratch, sems):
    copies = []
    for i, (axis, d, start, size, _) in enumerate(chunks):
        if axis == "x":
            into = scratch.at[lax.rem(x + d, NX), pl.ds(start, size)]
        else:
            into = scratch.at[pl.ds(start, size), lax.rem(z + d, NZ)]
        copies.append(pltpu.make_async_copy(refs[i], into, sems.at[i]))
    return copies


def project(acts, chunks, place_ids):
    tokens = acts.shape[1]
    rows, columns = chunks[0][4].shape[1:]

    def kernel(ids, acts_ref, *refs):
        sources = refs[: len(chunks)]
        out, weight, held, sems = refs[len(chunks) :]
        copies = weight_copies(chunks, sources, ids[0], ids[1], weight, sems)
        copies.append(pltpu.make_async_copy(acts_ref, held, sems.at[len(chunks)]))
        for copy in copies:
            copy.start()
        for copy in copies:
            copy.wait()
        out[...] = jnp.zeros_like(out)

        def step(b, carry):
            block = weight[b // 2, pl.ds((b % 2) * 4, 4)].reshape(4 * rows, columns)
            out[...] += jnp.dot(held[b], block, preferred_element_type=jnp.float32)
            return carry

        lax.fori_loop(0, 8, step, 0)

    return pl.pallas_call(
        kernel,
        out_shape=jax.ShapeDtypeStruct((tokens, columns), jnp.float32),
        in_specs=[SMEM, ANY] + [ANY] * len(chunks),
        out_specs=VMEM,
        scratch_shapes=[
            pltpu.VMEM((NX, NZ, rows, columns), jnp.bfloat16),
            pltpu.VMEM(acts.shape, jnp.bfloat16),
            pltpu.SemaphoreType.DMA((len(chunks) + 1,)),
        ],
        compiler_params=pltpu.CompilerParams(vmem_limit_bytes=VMEM_LIMIT),
        cost_estimate=pl.CostEstimate(
            flops=2 * tokens * 5120 * columns, bytes_accessed=9000000, transcendentals=0
        ),
    )(place_ids, acts, *[chunk[4] for chunk in chunks])


def output(pieces, chunks, place_ids):
    tokens, feats = pieces[0][2].shape
    rows = chunks[0][4].shape[1]

    def kernel(ids, *refs):
        sources = refs[: len(pieces)]
        weights = refs[len(pieces) : len(pieces) + len(chunks)]
        out, weight, held, total, sems = refs[len(pieces) + len(chunks) :]
        copies = weight_copies(chunks, weights, ids[0], ids[1], weight, sems)
        for i, (d, other, _) in enumerate(pieces):
            core = 1 - ids[3] if other else ids[3]
            slot = lax.rem(ids[2] + d, NY) * NC + core
            copies.append(
                pltpu.make_async_copy(sources[i], held.at[slot], sems.at[len(chunks) + i])
            )
        for copy in copies:
            copy.start()
        for copy in copies:
            copy.wait()
        total[...] = jnp.zeros_like(total)

        def step(b, carry):
            block = weight[b // 2, pl.ds((b % 2) * 4, 4)].reshape(4 * rows, feats)
            total[...] += lax.dot_general(
                held[b], block, (((1,), (1,)), ((), ())), preferred_element_type=jnp.float32
            )
            return carry

        lax.fori_loop(0, 8, step, 0)
        out[...] = total[...].astype(jnp.bfloat16)

    return pl.pallas_call(
        kernel,
        out_shape=jax.ShapeDtypeStruct((tokens, 4 * rows), jnp.bfloat16),
        in_specs=[SMEM] + [ANY] * (len(pieces) + len(chunks)),
        out_specs=VMEM,
        scratch_shapes=[
            pltpu.VMEM((NX, NZ, rows, feats), jnp.bfloat16),
            pltpu.VMEM((NY * NC, tokens, feats), jnp.bfloat16),
            pltpu.VMEM((tokens, 4 * rows), jnp.float32),
            pltpu.SemaphoreType.DMA((len(chunks) + len(pieces),)),
        ],
        compiler_params=pltpu.CompilerParams(vmem_limit_bytes=VMEM_LIMIT),
        cost_estimate=pl.CostEstimate(
            flops=2 * tokens * 3072 * 640, bytes_accessed=7000000, transcendentals=0
        ),
    )(place_ids, *[piece[2] for piece in pieces], *[chunk[4] for chunk in chunks])


def attention(query, keys, values, ids, count):
    tokens, feats = query.shape
    slots = ids.shape[0]
    heads = feats // HD
    scale = HD ** (-0.5)

    def kernel(ids_ref, count_ref, q_ref, *refs):
        sources, (out, k_held, v_held, sems) = refs[:6], refs[6:]
        copies = [
            pltpu.make_async_copy(
                sources[i], (k_held if i < 3 else v_held).at[i % 3], sems.at[i]
            )
            for i in range(6)
        ]
        for copy in copies:
            copy.start()
        for copy in copies:
            copy.wait()
        for h in range(heads):
            cols = slice(h * HD, (h + 1) * HD)
            q = q_ref[:, cols]
            scores = []
            for s in range(slots):
                key = k_held[ids_ref[s], :, cols]
                part = lax.dot_general(
                    q, key, (((1,), (1,)), ((), ())), preferred_element_type=jnp.float32
                )
                live = s < count_ref[0]
                scores.append(jnp.where(live, part * scale, masked_score))
            top = scores[0].max(axis=1, keepdims=True)
            for part in scores[1:]:
                top = jnp.maximum(top, part.max(axis=1, keepdims=True))
            weights = [jnp.exp(part - top) for part in scores]
            total = weights[0].sum(axis=1, keepdims=True)
            for part in weights[1:]:
                total = total + part.sum(axis=1, keepdims=True)
            inverse = 1.0 / total
            mixed = None
            for s in range(slots):
                probs = (weights[s] * inverse).astype(jnp.bfloat16)
                term = jnp.dot(
                    probs, v_held[ids_ref[s], :, cols], preferred_element_type=jnp.float32
                )
                mixed = term if mixed is None else mixed + term
            out[:, cols] = mixed.astype(jnp.bfloat16)

    return pl.pallas_call(
        kernel,
        out_shape=jax.ShapeDtypeStruct((tokens, feats), jnp.bfloat16),
        in_specs=[SMEM, SMEM, VMEM] + [ANY] * 6,
        out_specs=VMEM,
        scratch_shapes=[
            pltpu.VMEM((3, tokens, feats), jnp.bfloat16),
            pltpu.VMEM((3, tokens, feats), jnp.bfloat16),
            pltpu.SemaphoreType.DMA((6,)),
        ],
        compiler_params=pltpu.CompilerParams(vmem_limit_bytes=VMEM_LIMIT),
        cost_estimate=pl.CostEstimate(
            flops=4 * tokens * tokens * slots * feats,
            bytes_accessed=4000000,
            transcendentals=tokens * tokens * slots * heads,
        ),
    )(ids, count, query, *keys, *values)


def head_sum(part):
    part = part + to_sibling(part)
    return part + along_y(part, 1) + along_y(part, -1) + along_y(part, 2)


def normal(raw, gain, features):
    total = head_sum(jnp.sum(raw * raw, axis=1))
    return (raw * lax.rsqrt(total[:, None] / features + norm_eps) * gain).astype(jnp.bfloat16)


def shards(
    activations, w_query, w_key, w_value, query_gain, key_gain, w_output, kv_tiles, kv_count
):
    slab = lax.axis_index("slab")
    head = lax.axis_index("head")
    x, z, y, c = slab // NZ, slab % NZ, head // NC, head % NC
    place_ids = jnp.stack([x, z, y, c]).astype(jnp.int32)
    features = w_query.shape[1] * NY * NC

    near = [activations] + [along_y(activations, -d) for d in (1, 2, 3)]
    far = [to_sibling(piece) for piece in near]

    acts = gather_heads(near, far, place_ids)

    turned = moved(
        w_output.T, lambda x, z, y, c: (y, 4 * c + z % 4, x, z // 4)
    )

    key_chunks = gather_zx(w_key, x, z)
    value_chunks = gather_xz(w_value, x, z)
    query_chunks = gather_zx(w_query, x, z)
    output_chunks = gather_xz(turned, x, z)

    k_raw = project(acts, key_chunks, place_ids)
    key_tok = normal(k_raw, key_gain, features)
    keys = (along_slab(key_tok, 1), key_tok, along_slab(key_tok, -1))
    value_tok = project(acts, value_chunks, place_ids).astype(jnp.bfloat16)
    values = (along_slab(value_tok, 1), value_tok, along_slab(value_tok, -1))
    q_raw = project(acts, query_chunks, place_ids)
    query_tok = normal(q_raw, query_gain, features)

    local_ids = jnp.clip(kv_tiles[0] - slab + 1, 0, 2).astype(jnp.int32)
    attended = attention(query_tok, keys, values, local_ids, kv_count)

    mine = [attended] + [along_y(attended, -d) for d in (1, 2, 3)]
    theirs = [to_sibling(piece) for piece in mine]
    pieces = [(d, False, piece) for d, piece in enumerate(mine)]
    pieces += [(d, True, piece) for d, piece in enumerate(theirs)]
    return output(pieces, output_chunks, place_ids)


def gather_heads(near, far, place_ids):
    cells = near[0]

    def kernel(ids, *refs):
        sources, out, sems = refs[:8], refs[8], refs[9]
        copies = []
        for i in range(8):
            core = ids[3] if i < 4 else 1 - ids[3]
            slot = lax.rem(ids[2] + i % 4, NY) * NC + core
            copies.append(pltpu.make_async_copy(sources[i], out.at[slot], sems.at[i]))
        for copy in copies:
            copy.start()
        for copy in copies:
            copy.wait()

    return pl.pallas_call(
        kernel,
        out_shape=jax.ShapeDtypeStruct((NY * NC,) + cells.shape, cells.dtype),
        in_specs=[SMEM] + [ANY] * 8,
        out_specs=ANY,
        scratch_shapes=[pltpu.SemaphoreType.DMA((8,))],
        compiler_params=pltpu.CompilerParams(vmem_limit_bytes=VMEM_LIMIT),
    )(place_ids, *near, *far)


def solution(mesh):
    return jax.shard_map(
        shards,
        mesh=mesh,
        in_specs=(
            P("slab", "head"),
            P("slab", "head"),
            P("slab", "head"),
            P("slab", "head"),
            P("head"),
            P("head"),
            P("head", "slab"),
            P("slab", None),
            P("slab"),
        ),
        out_specs=P("slab", "head"),
        check_vma=False,
    )
```

```python
import jax
import jax.numpy as jnp
from jax import lax
from jax.experimental import pallas as pl
from jax.experimental.pallas import tpu as pltpu
from jax.sharding import PartitionSpec as P

HD = 128
NX, NZ, NY, NC = 4, 8, 4, 2

norm_eps = 1e-06
masked_score = -1e30
VMEM_LIMIT = 48 * 1024 * 1024
HBM = pl.BlockSpec(memory_space=pltpu.HBM)
SMEM = pl.BlockSpec(memory_space=pltpu.SMEM)
VMEM = pl.BlockSpec(memory_space=pltpu.VMEM)
PARAMS = pltpu.CompilerParams(vmem_limit_bytes=VMEM_LIMIT)


def group(x):
    return x // 2


def mate(x):
    return x ^ 1


def partner(x):
    return 3 - x


def device(x, z, y, c):
    return ((x * NZ + z) * NY + y) * NC + c


def moved(cells, target):
    pairs = []
    for x in range(NX):
        for z in range(NZ):
            for y in range(NY):
                for c in range(NC):
                    to = target(x, z, y, c)
                    if to is not None:
                        pairs.append((device(x, z, y, c), device(*to)))
    return lax.ppermute(cells, ("slab", "head"), pairs)


def along_x(cells, step):
    return moved(cells, lambda x, z, y, c: ((x + step) % NX, z, y, c))


def along_z(cells, step):
    return moved(cells, lambda x, z, y, c: (x, (z + step) % NZ, y, c))


def along_y(cells, step):
    return moved(cells, lambda x, z, y, c: (x, z, (y + step) % NY, c))


def to_sibling(cells):
    return moved(cells, lambda x, z, y, c: (x, z, y, 1 - c))


def to_partner(cells):
    return moved(cells, lambda x, z, y, c: (partner(x), z, y, c))


def both_ways(cells):
    return moved(cells, lambda x, z, y, c: (x, (z - 1 + 2 * c) % NZ, y, c))


def along_slab(cells, step):
    def target(x, z, y, c):
        slab_x = x if c == group(x) else partner(x)
        slab = (slab_x * NZ + z + step) % (NX * NZ)
        to_x = slab // NZ
        chip = to_x if group(to_x) == group(x) else partner(to_x)
        return (chip, slab % NZ, y, group(to_x))

    return moved(cells, target)


def first_shards(shard):
    return moved(
        shard,
        lambda x, z, y, c: (mate(x), z, y, c)
        if c == group(x)
        else (partner(x), z, y, group(x)),
    )


def second_shards(shard):
    return moved(
        shard, lambda x, z, y, c: None if c == group(x) else (x ^ 2, z, y, group(x))
    )


def ring(cells, shift, count):
    pieces = [None] * count
    pieces[0] = cells
    ahead, behind = cells, cells
    for step in range(1, count // 2):
        ahead = shift(ahead, -1)
        behind = shift(behind, 1)
        pieces[step] = ahead
        pieces[count - step] = behind
    half = cells.shape[0] // 2
    pieces[count // 2] = (shift(ahead[:half], -1), shift(behind[half:], 1))
    return pieces


def run(copies):
    for copy in copies:
        copy.start()
    for copy in copies:
        copy.wait()


def place(pieces, ids, which):
    count = len(pieces)
    cells = pieces[0]
    flat, where = [], []
    for d, piece in enumerate(pieces):
        if isinstance(piece, tuple):
            half = cells.shape[0] // 2
            flat += list(piece)
            where += [(d, 0, half), (d, half, half)]
        else:
            flat.append(piece)
            where.append((d, 0, cells.shape[0]))

    def kernel(ids_ref, *refs):
        sources, out, sems = refs[: len(flat)], refs[-2], refs[-1]
        copies = []
        for i, (d, start, size) in enumerate(where):
            slot = lax.rem(ids_ref[which] + d, count)
            copies.append(
                pltpu.make_async_copy(
                    sources[i], out.at[slot, pl.ds(start, size)], sems.at[i]
                )
            )
        run(copies)

    return pl.pallas_call(
        kernel,
        out_shape=jax.ShapeDtypeStruct((count,) + cells.shape, cells.dtype),
        in_specs=[SMEM] + [HBM] * len(flat),
        out_specs=VMEM,
        scratch_shapes=[pltpu.SemaphoreType.DMA((len(flat),))],
        compiler_params=PARAMS,
    )(ids, *flat)


def gather_zx(cells, ids):
    own = place(ring(cells, along_z, NZ), ids, 1)
    chunks = []
    for d, piece in enumerate(ring(own, along_x, NX)):
        if isinstance(piece, tuple):
            chunks += [(d, 0, NZ // 2, piece[0]), (d, NZ // 2, NZ // 2, piece[1])]
        else:
            chunks.append((d, 0, NZ, piece))
    return chunks


def arrange(near, far, ids):
    tokens, width = near[0].shape
    block = width // 4

    def kernel(ids_ref, *refs):
        sources, (out, held, sems) = refs[:8], refs[8:]
        copies = []
        for i in range(8):
            core = ids_ref[3] if i < 4 else 1 - ids_ref[3]
            slot = lax.rem(ids_ref[2] + i % 4, NY)
            copies.append(pltpu.make_async_copy(sources[i], held.at[slot, core], sems.at[i]))
        run(copies)
        x = ids_ref[0]
        mate_x = x + 1 - 2 * lax.rem(x, 2)
        order = [x, mate_x, 3 - x, 3 - mate_x]
        for j in range(NX):
            for core in range(NC):
                for low in range(4):
                    out[4 * core + low, :, j * block : (j + 1) * block] = held[
                        order[j], core, :, low * block : (low + 1) * block
                    ]

    return pl.pallas_call(
        kernel,
        out_shape=jax.ShapeDtypeStruct((NZ, tokens, NX * block), near[0].dtype),
        in_specs=[SMEM] + [HBM] * 8,
        out_specs=VMEM,
        scratch_shapes=[
            pltpu.VMEM((NY, NC, tokens, width), near[0].dtype),
            pltpu.SemaphoreType.DMA((8,)),
        ],
        compiler_params=PARAMS,
    )(ids, *near, *far)


def accumulate(total, acts, groups, ids):
    tokens, width = acts.shape[1:]
    columns = groups[0][1][0][3].shape[-1]
    rows = groups[0][1][0][3].shape[-2]
    chunks = [(i,) + chunk for i, (_, members) in enumerate(groups) for chunk in members]
    first = total is None

    def kernel(ids_ref, acts_ref, *refs):
        sources = refs[: len(chunks)]
        rest = refs[len(chunks) :]
        if not first:
            before, rest = rest[0], rest[1:]
        out, weight, held, sems = rest
        sign = 1 - 2 * ids_ref[3]
        copies = []
        for k, (i, opposite, start, size, _) in enumerate(chunks):
            kind = 1 - ids_ref[4] if opposite else ids_ref[4]
            if start is None:
                begin = 2 * kind
            else:
                begin = 2 * kind + (1 - ids_ref[3] if start else ids_ref[3])
            copies.append(
                pltpu.make_async_copy(
                    sources[k], weight.at[i, pl.ds(begin, size)], sems.at[k]
                )
            )
        for i, (distance, _) in enumerate(groups):
            slot = lax.rem(ids_ref[1] + sign * distance + NZ, NZ)
            copies.append(
                pltpu.make_async_copy(acts_ref.at[slot], held.at[i], sems.at[len(chunks) + i])
            )
        run(copies)
        for i in range(len(groups)):
            term = jnp.dot(
                held[i],
                weight[i].reshape(NX * rows, columns),
                preferred_element_type=jnp.float32,
            )
            if i:
                out[...] += term
            elif first:
                out[...] = term
            else:
                out[...] = before[...] + term

    return pl.pallas_call(
        kernel,
        out_shape=jax.ShapeDtypeStruct((tokens, columns), jnp.float32),
        in_specs=[SMEM, HBM] + [HBM] * len(chunks) + ([] if first else [VMEM]),
        out_specs=VMEM,
        scratch_shapes=[
            pltpu.VMEM((len(groups), NX, rows, columns), jnp.bfloat16),
            pltpu.VMEM((len(groups), tokens, width), jnp.bfloat16),
            pltpu.SemaphoreType.DMA((len(chunks) + len(groups),)),
        ],
        compiler_params=PARAMS,
        cost_estimate=pl.CostEstimate(
            flops=2 * tokens * width * columns * len(groups),
            bytes_accessed=3000000 * len(groups),
            transcendentals=0,
        ),
    )(ids, acts, *[chunk[4] for chunk in chunks], *([] if first else [total]))


def output(pieces, chunks, ids):
    tokens, feats = pieces[0][2].shape
    rows = chunks[0][3].shape[1]

    def kernel(ids_ref, *refs):
        sources = refs[: len(pieces)]
        weights = refs[len(pieces) : len(pieces) + len(chunks)]
        out, weight, held, total, sems = refs[len(pieces) + len(chunks) :]
        copies = []
        for i, (d, start, size, _) in enumerate(chunks):
            into = weight.at[lax.rem(ids_ref[0] + d, NX), pl.ds(start, size)]
            copies.append(pltpu.make_async_copy(weights[i], into, sems.at[i]))
        for i, (d, other, _) in enumerate(pieces):
            core = 1 - ids_ref[3] if other else ids_ref[3]
            slot = lax.rem(ids_ref[2] + d, NY) * NC + core
            copies.append(
                pltpu.make_async_copy(sources[i], held.at[slot], sems.at[len(chunks) + i])
            )
        run(copies)
        total[...] = jnp.zeros_like(total)

        def step(b, carry):
            block = weight[b // 2, pl.ds((b % 2) * 4, 4)].reshape(4 * rows, feats)
            total[...] += lax.dot_general(
                held[b], block, (((1,), (1,)), ((), ())), preferred_element_type=jnp.float32
            )
            return carry

        lax.fori_loop(0, 8, step, 0)
        out[...] = total[...].astype(jnp.bfloat16)

    return pl.pallas_call(
        kernel,
        out_shape=jax.ShapeDtypeStruct((tokens, 4 * rows), jnp.bfloat16),
        in_specs=[SMEM] + [HBM] * (len(pieces) + len(chunks)),
        out_specs=VMEM,
        scratch_shapes=[
            pltpu.VMEM((NX, NZ, rows, feats), jnp.bfloat16),
            pltpu.VMEM((NY * NC, tokens, feats), jnp.bfloat16),
            pltpu.VMEM((tokens, 4 * rows), jnp.float32),
            pltpu.SemaphoreType.DMA((len(chunks) + len(pieces),)),
        ],
        compiler_params=PARAMS,
        cost_estimate=pl.CostEstimate(
            flops=2 * tokens * 3072 * 640, bytes_accessed=7000000, transcendentals=0
        ),
    )(ids, *[piece[2] for piece in pieces], *[chunk[3] for chunk in chunks])


def attention(query, sides, factors, local_ids, count):
    tokens, feats = query.shape
    slots = local_ids.shape[0]
    heads = feats // HD

    def kernel(ids_ref, count_ref, q_ref, factor_ref, *refs):
        sources, (out, held, sems) = refs[:3], refs[3:]
        run([pltpu.make_async_copy(sources[i], held.at[i], sems.at[i]) for i in range(3)])
        for h in range(heads):
            q = q_ref[:, h * HD : (h + 1) * HD]
            scores = []
            for s in range(slots):
                key = held[ids_ref[s], :, h * HD : (h + 1) * HD]
                part = lax.dot_general(
                    q, key, (((1,), (1,)), ((), ())), preferred_element_type=jnp.float32
                )
                live = s < count_ref[0]
                scores.append(jnp.where(live, part * factor_ref[ids_ref[s]], masked_score))
            top = scores[0].max(axis=1, keepdims=True)
            for part in scores[1:]:
                top = jnp.maximum(top, part.max(axis=1, keepdims=True))
            weights = [jnp.exp(part - top) for part in scores]
            total = weights[0].sum(axis=1, keepdims=True)
            for part in weights[1:]:
                total = total + part.sum(axis=1, keepdims=True)
            inverse = 1.0 / total
            mixed = None
            for s in range(slots):
                probs = (weights[s] * inverse).astype(jnp.bfloat16)
                value = held[ids_ref[s], :, feats + h * HD : feats + (h + 1) * HD]
                term = jnp.dot(probs, value, preferred_element_type=jnp.float32)
                mixed = term if mixed is None else mixed + term
            out[:, h * HD : (h + 1) * HD] = mixed.astype(jnp.bfloat16)

    return pl.pallas_call(
        kernel,
        out_shape=jax.ShapeDtypeStruct((tokens, feats), jnp.bfloat16),
        in_specs=[SMEM, SMEM, VMEM, VMEM] + [HBM] * 3,
        out_specs=VMEM,
        scratch_shapes=[
            pltpu.VMEM((3, tokens, 2 * feats), jnp.bfloat16),
            pltpu.SemaphoreType.DMA((3,)),
        ],
        compiler_params=PARAMS,
        cost_estimate=pl.CostEstimate(
            flops=4 * tokens * tokens * slots * feats,
            bytes_accessed=4000000,
            transcendentals=tokens * tokens * slots * heads,
        ),
    )(local_ids, count, query, factors, *sides)


def shards(
    activations, w_query, w_key, w_value, query_gain, key_gain, w_output, kv_tiles, kv_count
):
    slab = lax.axis_index("slab")
    head = lax.axis_index("head")
    x, z, y, c = slab // NZ, slab % NZ, head // NC, head % NC
    home = c == x // 2
    kind = jnp.where(home, 0, 1)
    ids = jnp.stack([x, z, y, c, kind]).astype(jnp.int32)
    feats = w_query.shape[1]
    features = feats * NY * NC

    gains = jnp.stack([query_gain, key_gain])
    gains = jnp.where(home, gains, to_sibling(gains))
    lists = jnp.concatenate([kv_tiles[0], kv_count])
    lists = jnp.where(home, lists, to_partner(lists))
    slab_here = jnp.where(home, x, 3 - x) * NZ + z

    near = moved(
        activations,
        lambda x, z, y, c: (partner(x), z, y, c) if c == group(x) else (x, z, y, group(x)),
    )
    far = moved(
        activations,
        lambda x, z, y, c: None if c == group(x) else (partner(x), z, y, group(x)),
    )
    first = jnp.where(home, activations, near)
    second = jnp.where(home, near, far)
    first_up, second_up = along_y(first, -1), along_y(second, -1)
    first_down, second_down = along_y(first, 1), along_y(second, 1)
    first_far, second_far = along_y(first_up, -1), along_y(second_down, 1)
    acts = arrange(
        [first, first_up, first_far, first_down],
        [second, second_up, second_far, second_down],
        ids,
    )

    shard = jnp.concatenate([w_query, w_key, w_value], axis=1)
    got = first_shards(shard)
    got_far = second_shards(shard)
    mine = jnp.where(home, jnp.stack([shard, got]), jnp.stack([got, got_far]))
    other = to_sibling(mine)
    total = None
    groups = [(0, [(False, None, 2, mine), (True, None, 2, other)])]
    near_chain, far_chain = mine, other
    rounds = [groups]
    for step in (1, 2, 3):
        near_chain, far_chain = both_ways(near_chain), both_ways(far_chain)
        near_swap, far_swap = to_sibling(near_chain), to_sibling(far_chain)
        rounds.append(
            [
                (step, [(False, None, 2, near_chain), (True, None, 2, far_chain)]),
                (-step, [(True, None, 2, near_swap), (False, None, 2, far_swap)]),
            ]
        )
    near_half = both_ways(lax.dynamic_slice_in_dim(near_chain, c, 1, 0))
    far_half = both_ways(lax.dynamic_slice_in_dim(far_chain, c, 1, 0))
    near_swap, far_swap = to_sibling(near_half), to_sibling(far_half)
    rounds.append(
        [
            (
                4,
                [
                    (False, 0, 1, near_half),
                    (True, 0, 1, far_half),
                    (True, 1, 1, near_swap),
                    (False, 1, 1, far_swap),
                ],
            )
        ]
    )

    turned = moved(w_output.T, lambda x, z, y, c: (y, 4 * c + z % 4, x, z // 4))
    output_chunks = gather_zx(turned, ids)

    for groups in rounds:
        total = accumulate(total, acts, groups, ids)

    q_raw, k_raw, v_raw = total[:, :feats], total[:, feats : 2 * feats], total[:, 2 * feats :]
    sums = jnp.stack([jnp.sum(q_raw * q_raw, axis=1), jnp.sum(k_raw * k_raw, axis=1)])
    sides = jnp.concatenate([k_raw * gains[1], v_raw], axis=1).astype(jnp.bfloat16)
    sides = (along_slab(sides, 1), sides, along_slab(sides, -1))
    sums = sums + to_partner(sums)
    sums = sums + along_y(sums, 1) + along_y(sums, -1) + along_y(sums, 2)
    norms = lax.rsqrt(sums / features + norm_eps)
    query = (q_raw * norms[0][:, None] * gains[0]).astype(jnp.bfloat16)
    factor = norms[1] * HD ** (-0.5)
    factors = jnp.stack([along_slab(factor, 1), factor, along_slab(factor, -1)])[:, None, :]

    local_ids = jnp.clip(lists[:3] - slab_here + 1, 0, 2).astype(jnp.int32)
    attended = attention(query, sides, factors, local_ids, lists[3:])

    pieces = []
    for d in range(NY):

        def target(x, z, y, c, d=d):
            if c == group(x):
                return (x, z, (y + d) % NY, c) if d else None
            return (partner(x), z, (y + d) % NY, group(x))

        piece = moved(attended, target)
        if d == 0:
            piece = jnp.where(home, attended, piece)
        pieces.append(((NY - d) % NY, False, piece))
    pieces += [(d, True, to_sibling(piece)) for d, _, piece in pieces]
    return output(pieces, output_chunks, ids)


def solution(mesh):
    return jax.shard_map(
        shards,
        mesh=mesh,
        in_specs=(
            P("slab", "head"),
            P("slab", "head"),
            P("slab", "head"),
            P("slab", "head"),
            P("head"),
            P("head"),
            P("head", "slab"),
            P("slab", None),
            P("slab"),
        ),
        out_specs=P("slab", "head"),
        check_vma=False,
    )
```

```python
import jax
import jax.numpy as jnp
from jax import lax
from jax.experimental import pallas as pl
from jax.experimental.pallas import tpu as pltpu
from jax.sharding import PartitionSpec as P

HD = 128
NX, NZ, NY, NC = 4, 8, 4, 2

norm_eps = 1e-06
masked_score = -1e30
ANY = pl.BlockSpec(memory_space=pl.ANY)
HBM = pl.BlockSpec(memory_space=pltpu.HBM)
SMEM = pl.BlockSpec(memory_space=pltpu.SMEM)
VMEM = pl.BlockSpec(memory_space=pltpu.VMEM)
LARGE = pltpu.CompilerParams(vmem_limit_bytes=16 * 1024 * 1024)
MEDIUM = pltpu.CompilerParams(vmem_limit_bytes=12 * 1024 * 1024)
WHOLE = pltpu.CompilerParams(vmem_limit_bytes=60 * 1024 * 1024)
SMALL = pltpu.CompilerParams(vmem_limit_bytes=4 * 1024 * 1024)
TINY = pltpu.CompilerParams(vmem_limit_bytes=1024 * 1024)
LIGHT = pl.CostEstimate(flops=1, bytes_accessed=1, transcendentals=0)

BLOCKS = (0, 2, 5)
FREE = 4


def group(x):
    return x // 2


def mate(x):
    return x ^ 1


def partner(x):
    return 3 - x


def device(x, z, y, c):
    return ((x * NZ + z) * NY + y) * NC + c


def moved(cells, target):
    pairs = []
    for x in range(NX):
        for z in range(NZ):
            for y in range(NY):
                for c in range(NC):
                    to = target(x, z, y, c)
                    if to is not None:
                        pairs.append((device(x, z, y, c), device(*to)))
    return lax.ppermute(cells, ("slab", "head"), pairs)


def along_x(cells, step):
    return moved(cells, lambda x, z, y, c: ((x + step) % NX, z, y, c))


def along_z(cells, step):
    return moved(cells, lambda x, z, y, c: (x, (z + step) % NZ, y, c))


def along_y(cells, step):
    return moved(cells, lambda x, z, y, c: (x, z, (y + step) % NY, c))


def to_sibling(cells):
    return moved(cells, lambda x, z, y, c: (x, z, y, 1 - c))


def to_partner(cells):
    return moved(cells, lambda x, z, y, c: (partner(x), z, y, c))


def along_slab(cells, step):
    def target(x, z, y, c):
        slab_x = x if c == group(x) else partner(x)
        slab = (slab_x * NZ + z + step) % (NX * NZ)
        to_x = slab // NZ
        chip = to_x if group(to_x) == group(x) else partner(to_x)
        return (chip, slab % NZ, y, group(to_x))

    return moved(cells, target)


def first_shards(shard):
    return moved(
        shard,
        lambda x, z, y, c: (mate(x), z, y, c)
        if c == group(x)
        else (partner(x), z, y, group(x)),
    )


def second_shards(shard):
    return moved(
        shard, lambda x, z, y, c: None if c == group(x) else (x ^ 2, z, y, group(x))
    )


def together(*arrays):
    return lax.optimization_barrier(arrays)


def run(copies):
    for copy in copies:
        copy.start()
    for copy in copies:
        copy.wait()


def join(cells):
    def kernel(*refs):
        out, sems = refs[len(cells) :]
        run([pltpu.make_async_copy(refs[i], out.at[i], sems.at[i]) for i in range(len(cells))])

    return pl.pallas_call(
        kernel,
        out_shape=jax.ShapeDtypeStruct((len(cells),) + cells[0].shape, cells[0].dtype),
        in_specs=[HBM] * len(cells),
        out_specs=VMEM,
        scratch_shapes=[pltpu.SemaphoreType.DMA((len(cells),))],
        compiler_params=WHOLE,
        cost_estimate=LIGHT,
    )(*cells)


def pack(shard, got, got_far, turned, ids):
    kinds = shard.shape[0]

    def kernel(ids_ref, shard_ref, got_ref, far_ref, turned_ref, out, sems):
        free = pltpu.make_async_copy(turned_ref, out.at[FREE], sems.at[2 * kinds])
        free.start()

        def fill(one, two):
            copies = []
            for w in range(kinds):
                for j, source in enumerate((one, two)):
                    copies.append(
                        pltpu.make_async_copy(
                            source.at[w], out.at[BLOCKS[w] + j], sems.at[2 * w + j]
                        )
                    )
            run(copies)

        @pl.when(ids_ref[4] == 0)
        def _():
            fill(shard_ref, got_ref)

        @pl.when(ids_ref[4] != 0)
        def _():
            fill(got_ref, far_ref)

        free.wait()

    return pl.pallas_call(
        kernel,
        out_shape=jax.ShapeDtypeStruct((2 * kinds + 1,) + shard.shape[1:], shard.dtype),
        in_specs=[SMEM] + [ANY] * 4,
        out_specs=VMEM,
        scratch_shapes=[pltpu.SemaphoreType.DMA((2 * kinds + 1,))],
        compiler_params=SMALL,
        cost_estimate=LIGHT,
    )(ids, shard, got, got_far, turned)


def collect(pieces):
    cells = pieces[0][0]

    def kernel(*refs):
        out, sems = refs[len(pieces) :]
        copies = []
        for i, (_, index) in enumerate(pieces):
            copies.append(pltpu.make_async_copy(refs[i].at[index], out.at[i], sems.at[i]))
        run(copies)

    return pl.pallas_call(
        kernel,
        out_shape=jax.ShapeDtypeStruct((len(pieces),) + cells.shape[-2:], cells.dtype),
        in_specs=[ANY] * len(pieces),
        out_specs=VMEM,
        scratch_shapes=[pltpu.SemaphoreType.DMA((len(pieces),))],
        compiler_params=TINY,
        cost_estimate=LIGHT,
    )(*[piece[0] for piece in pieces])


def arrange(own, swapped, ids):
    tokens, width = own[0].shape
    block = width // 4

    def kernel(ids_ref, *refs):
        sources, swapped_ref, (out, held, sems) = refs[:NY], refs[NY], refs[NY + 1 :]
        copies = []
        for d in range(NY):
            slot = lax.rem(ids_ref[2] + d, NY)
            copies.append(
                pltpu.make_async_copy(sources[d], held.at[slot, ids_ref[3]], sems.at[d])
            )
            copies.append(
                pltpu.make_async_copy(
                    swapped_ref.at[d], held.at[slot, 1 - ids_ref[3]], sems.at[NY + d]
                )
            )
        run(copies)
        x = ids_ref[0]
        mate_x = x + 1 - 2 * lax.rem(x, 2)
        order = [x, mate_x, 3 - x, 3 - mate_x]
        for j in range(NX):
            for core in range(NC):
                for low in range(4):
                    out[4 * core + low, :, j * block : (j + 1) * block] = held[
                        order[j], core, :, low * block : (low + 1) * block
                    ]

    return pl.pallas_call(
        kernel,
        out_shape=jax.ShapeDtypeStruct((NZ, tokens, NX * block), own[0].dtype),
        in_specs=[SMEM] + [ANY] * (NY + 1),
        out_specs=VMEM,
        scratch_shapes=[
            pltpu.VMEM((NY, NC, tokens, width), own[0].dtype),
            pltpu.SemaphoreType.DMA((2 * NY,)),
        ],
        compiler_params=LARGE,
        cost_estimate=LIGHT,
    )(ids, *own, swapped)


def accumulate(total, acts, groups, ids):
    tokens, width = acts.shape[1:]
    rows, feats = groups[0][1][0][1].shape[1:]
    columns = 3 * feats
    chunks = [(i,) + chunk for i, (_, members) in enumerate(groups) for chunk in members]
    slots = len(groups) + sum(len(chunk[3]) for chunk in chunks)
    first = total is None

    def kernel(ids_ref, acts_ref, *refs):
        sources = refs[: len(chunks)]
        rest = refs[len(chunks) :]
        if not first:
            before, rest = rest[0], rest[1:]
        out, weight, held, sems = rest
        copies = [[] for _ in groups]
        used = 0
        for i, (distance, _) in enumerate(groups):
            slot = lax.rem(ids_ref[1] + distance, NZ)
            copies[i].append(pltpu.make_async_copy(acts_ref.at[slot], held.at[i], sems.at[used]))
            used += 1
        for k, (i, opposite, _, parts) in enumerate(chunks):
            kind = 1 - ids_ref[4] if opposite else ids_ref[4]
            for w, begin in parts:
                into = weight.at[i, pl.ds(2 * kind, 2), :, w * feats : (w + 1) * feats]
                copies[i].append(
                    pltpu.make_async_copy(sources[k].at[pl.ds(begin, 2)], into, sems.at[used])
                )
                used += 1
        for members in copies:
            for copy in members:
                copy.start()
        for i in range(len(groups)):
            for copy in copies[i]:
                copy.wait()
            term = jnp.dot(
                held[i],
                weight[i].reshape(NX * rows, columns),
                preferred_element_type=jnp.float32,
            )
            if i:
                out[...] += term
            elif first:
                out[...] = term
            else:
                out[...] = before[...] + term

    return pl.pallas_call(
        kernel,
        out_shape=jax.ShapeDtypeStruct((tokens, columns), jnp.float32),
        in_specs=[SMEM, ANY] + [ANY] * len(chunks) + ([] if first else [VMEM]),
        out_specs=VMEM,
        scratch_shapes=[
            pltpu.VMEM((len(groups), NX, rows, columns), jnp.bfloat16),
            pltpu.VMEM((len(groups), tokens, width), jnp.bfloat16),
            pltpu.SemaphoreType.DMA((slots,)),
        ],
        compiler_params=MEDIUM,
        cost_estimate=LIGHT,
    )(ids, acts, *[chunk[2] for chunk in chunks], *([] if first else [total]))


def output(pieces, chunks, other, kind, ids):
    feats = pieces[0][2].shape[1]
    tokens = pieces[0][2].shape[0]
    rows = chunks[0][2].shape[1]
    blocks = [
        (k, i, far, d)
        for k, (far, distances, _) in enumerate(chunks)
        for i, d in enumerate(distances)
        if d is not None
    ]

    def kernel(ids_ref, *refs):
        sources, refs = refs[: len(pieces)], refs[len(pieces) :]
        weights, (out, weight, held, sems) = refs[: len(chunks)], refs[len(chunks) :]
        half = 1 - ids_ref[3] if other else ids_ref[3]

        def columns(slot):
            return pl.ds(pl.multiple_of(slot * feats, HD), feats)

        copies = []
        for i, (d, start, cells) in enumerate(pieces):
            slot = lax.rem(ids_ref[2] + d, NY)
            into = held.at[pl.ds(start, cells.shape[0]), columns(slot)]
            copies.append(pltpu.make_async_copy(sources[i], into, sems.at[i]))
        for copy in copies:
            copy.start()

        def each_block(act):
            for used, (k, i, far, d) in enumerate(blocks):
                z = lax.rem(ids_ref[1] + d, NZ)

                @pl.when(z // 4 == half)
                def _(used=used, k=k, i=i, far=far, z=z):
                    x = lax.rem(ids_ref[0] + far, NX)
                    into = weight.at[lax.rem(z, 4), :, columns(x)]
                    act(
                        pltpu.make_async_copy(
                            weights[k].at[i], into, sems.at[len(pieces) + used]
                        )
                    )

        each_block(lambda copy: copy.start())
        for copy in copies:
            copy.wait()
        each_block(lambda copy: copy.wait())
        out[...] = lax.dot_general(
            held[...],
            weight[...].reshape(4 * rows, NX * feats),
            (((1,), (1,)), ((), ())),
            preferred_element_type=jnp.float32,
        ).astype(kind)

    return pl.pallas_call(
        kernel,
        out_shape=jax.ShapeDtypeStruct((tokens, 4 * rows), kind),
        in_specs=[SMEM] + [ANY] * (len(pieces) + len(chunks)),
        out_specs=VMEM,
        scratch_shapes=[
            pltpu.VMEM((4, rows, NX * feats), jnp.bfloat16),
            pltpu.VMEM((tokens, NY * feats), jnp.bfloat16),
            pltpu.SemaphoreType.DMA((len(pieces) + len(blocks),)),
        ],
        compiler_params=MEDIUM,
        cost_estimate=LIGHT,
    )(ids, *[piece[2] for piece in pieces], *[chunk[2] for chunk in chunks])


def attention(query, sides, factors, local_ids, count):
    tokens, feats = query.shape
    slots = local_ids.shape[0]
    heads = feats // HD

    def kernel(ids_ref, count_ref, q_ref, factor_ref, *refs):
        sources, (out, held, sems) = refs[:3], refs[3:]
        run([pltpu.make_async_copy(sources[i], held.at[i], sems.at[i]) for i in range(3)])
        for h in range(heads):
            q = q_ref[:, h * HD : (h + 1) * HD]
            scores = []
            for s in range(slots):
                key = held[ids_ref[s], :, h * HD : (h + 1) * HD]
                part = lax.dot_general(
                    q, key, (((1,), (1,)), ((), ())), preferred_element_type=jnp.float32
                )
                live = s < count_ref[0]
                scores.append(jnp.where(live, part * factor_ref[ids_ref[s]], masked_score))
            top = scores[0].max(axis=1, keepdims=True)
            for part in scores[1:]:
                top = jnp.maximum(top, part.max(axis=1, keepdims=True))
            weights = [jnp.exp(part - top) for part in scores]
            total = weights[0].sum(axis=1, keepdims=True)
            for part in weights[1:]:
                total = total + part.sum(axis=1, keepdims=True)
            inverse = 1.0 / total
            mixed = None
            for s in range(slots):
                probs = (weights[s] * inverse).astype(jnp.bfloat16)
                value = held[ids_ref[s], :, feats + h * HD : feats + (h + 1) * HD]
                term = jnp.dot(probs, value, preferred_element_type=jnp.float32)
                mixed = term if mixed is None else mixed + term
            out[:, h * HD : (h + 1) * HD] = mixed.astype(jnp.bfloat16)

    return pl.pallas_call(
        kernel,
        out_shape=jax.ShapeDtypeStruct((tokens, feats), jnp.bfloat16),
        in_specs=[SMEM, SMEM, VMEM, VMEM] + [ANY] * 3,
        out_specs=VMEM,
        scratch_shapes=[
            pltpu.VMEM((3, tokens, 2 * feats), jnp.bfloat16),
            pltpu.SemaphoreType.DMA((3,)),
        ],
        compiler_params=LARGE,
        cost_estimate=LIGHT,
    )(local_ids, count, query, factors, *sides)


def shards(
    activations, w_query, w_key, w_value, query_gain, key_gain, w_output, kv_tiles, kv_count
):
    slab = lax.axis_index("slab")
    head = lax.axis_index("head")
    x, z, y, c = slab // NZ, slab % NZ, head // NC, head % NC
    home = c == x // 2
    kind = jnp.where(home, 0, 1)
    ids = jnp.stack([x, z, y, c, kind]).astype(jnp.int32)
    feats = w_query.shape[1]
    features = feats * NY * NC

    whole = tuple(enumerate(BLOCKS))
    half = activations.shape[0] // 2

    def pair_of_chunks(cells, swapped, parts):
        return [(False, cells, parts), (True, swapped, parts)]

    def groups_of(step, ahead, behind, ahead_swapped, behind_swapped):
        return [
            (step, pair_of_chunks(ahead, ahead_swapped, whole)),
            (NZ - step, pair_of_chunks(behind, behind_swapped, whole)),
        ]

    shard = join([w_query, w_key, w_value])
    turned = moved(w_output.T, lambda x, z, y, c: (y, z, x, 1 - c))
    got, got_far, own_1, own_3, turned = together(
        first_shards(shard),
        second_shards(shard),
        along_y(activations, -1),
        along_y(activations, 1),
        to_sibling(turned),
    )
    mine = pack(shard, got, got_far, turned, ids)

    mine, own_0, own_1, own_3 = together(mine, activations, own_1, own_3)
    gains = jnp.stack([query_gain, key_gain])
    lists = jnp.concatenate([kv_tiles[0], kv_count])
    own_2a, own_2b, pair_0, gains, lists = together(
        along_y(own_1[:half], -1), along_y(own_3[half:], 1), to_partner(own_0), gains, lists
    )
    ahead_1, behind_1, own_2a, own_2b, pair_0, gains_got, lists_got = together(
        along_z(mine, -1),
        along_z(mine, 1),
        own_2a,
        own_2b,
        pair_0,
        to_sibling(gains),
        to_partner(lists),
    )
    gains = jnp.where(home, gains, gains_got)
    lists = jnp.where(home, lists, lists_got)
    slab_here = jnp.where(home, x, 3 - x) * NZ + z

    own_2 = jnp.concatenate([own_2a, own_2b])
    pair_1, pair_3 = along_y(pair_0, -1), along_y(pair_0, 1)
    early = together(mine, ahead_1, behind_1, pair_1, pair_3)
    ahead_2, behind_2, pair_1, pair_3, pair_2, mine_s, ahead_1s, behind_1s = together(
        along_z(ahead_1, -1),
        along_z(behind_1, 1),
        pair_1,
        pair_3,
        to_partner(own_2),
        to_sibling(early[0]),
        to_sibling(early[1]),
        to_sibling(early[2]),
    )

    owns = (own_0, own_1, own_2, own_3)
    pairs = (pair_0, pair_1, pair_2, pair_3)
    kept = [jnp.where(home, own, pair) for own, pair in zip(owns, pairs)]
    sent = jnp.stack([jnp.where(home, pair, own) for own, pair in zip(owns, pairs)])
    swapped = to_sibling(sent)
    acts = arrange(kept, swapped, ids)
    total = accumulate(None, acts, [(0, pair_of_chunks(mine, mine_s, whole))], ids)
    total = accumulate(total, acts, groups_of(1, ahead_1, behind_1, ahead_1s, behind_1s), ids)
    late = together(ahead_2, behind_2, swapped)
    ahead_3, behind_3, ahead_2s, behind_2s, total = together(
        along_z(ahead_2, -1),
        along_z(behind_2, 1),
        to_sibling(late[0]),
        to_sibling(late[1]),
        total,
    )

    ahead_3s, behind_3s = to_sibling(ahead_3), to_sibling(behind_3)
    total = accumulate(total, acts, groups_of(2, ahead_2, behind_2, ahead_2s, behind_2s), ids)
    out_first = collect([(cells, FREE) for cells in (mine, ahead_1, behind_1, ahead_2, behind_2)])
    out_first = together(out_first, ahead_3s, behind_3s)[0]
    total = accumulate(total, acts, groups_of(3, ahead_3, behind_3, ahead_3s, behind_3s), ids)
    ahead_4, behind_4, out_ahead_1, out_behind_1, total = together(
        along_z(ahead_3[:FREE], -1),
        along_z(behind_3[FREE:], 1),
        along_x(out_first, -1),
        along_x(out_first, 1),
        total,
    )
    members = pair_of_chunks(ahead_4, to_sibling(ahead_4), whole[:2])
    members += pair_of_chunks(behind_4, to_sibling(behind_4), ((2, 1),))
    total = accumulate(total, acts, [(4, members)], ids)

    q_raw, k_raw, v_raw = total[:, :feats], total[:, feats : 2 * feats], total[:, 2 * feats :]
    sums = jnp.stack([jnp.sum(q_raw * q_raw, axis=1), jnp.sum(k_raw * k_raw, axis=1)])
    sides = jnp.concatenate([k_raw * gains[1], v_raw], axis=1).astype(jnp.bfloat16)
    sums, sides = together(sums, sides)
    side_before, side_next = along_slab(sides, 1), along_slab(sides, -1)
    sums = sum(together(sums, along_y(sums, 1), along_y(sums, -1), along_y(sums, 2)))
    sums = sums + to_partner(sums)
    norms = lax.rsqrt(sums / features + norm_eps)
    query = (q_raw * norms[0][:, None] * gains[0]).astype(jnp.bfloat16)
    factor = norms[1] * HD ** (-0.5)
    factor, side_before, side_next = together(factor, side_before, side_next)
    factor_before, factor_next = together(along_slab(factor, 1), along_slab(factor, -1))

    first, second = (0, 1, 7, 2, 6), (3, 5, 4)
    out_second = collect([(ahead_3, FREE), (behind_3, FREE), (behind_4, 0)])
    out_up = collect(
        [(out_ahead_1, i) for i in range(3)] + [(out_second, i) for i in range(3)]
    )
    out_down = collect(
        [(out_behind_1, i) for i in range(3, 5)] + [(out_second, i) for i in range(3)]
    )
    out_up, out_down = together(out_up, out_down, sums)[:2]
    out_up, out_down = along_x(out_up, -1), along_x(out_down, 1)
    chunks = [(0, first, out_first), (1, first, out_ahead_1), (3, first, out_behind_1)]
    chunks += [(2, first[:3] + (None,) * 3, out_up), (2, first[3:] + (None,) * 3, out_down)]
    chunks += [(0, second, out_second)]
    chunks += [(1, (None,) * 3 + second, out_up), (3, (None,) * 2 + second, out_down)]
    factors = jnp.stack([factor_before, factor, factor_next])[:, None, :]
    local_ids = jnp.clip(lists[:3] - slab_here + 1, 0, 2).astype(jnp.int32)
    attended = attention(
        query,
        (side_before, sides, side_next),
        factors,
        local_ids,
        lists[3:],
    )

    pieces = [None] * NY
    for d in (0, 1, 3):

        def target(x, z, y, c, d=d):
            if c == group(x):
                return (x, z, (y + d) % NY, c) if d else None
            return (partner(x), z, (y + d) % NY, group(x))

        pieces[-d % NY] = moved(attended, target)
    near, up, down, out_up, out_down = together(
        pieces[0], pieces[1], pieces[3], out_up[3:5], out_down[4:]
    )
    far_1, far_2, out_far_1, out_far_2 = together(
        along_y(up[:half], -1),
        along_y(down[half:], 1),
        along_x(out_up, -1),
        along_x(out_down, 1),
    )
    near = jnp.where(home, attended, near)
    pieces = [(0, 0, near), (1, 0, up), (3, 0, down), (2, 0, far_1), (2, half, far_2)]
    chunks += [(2, second[:2], out_far_1), (2, second[2:], out_far_2)]
    sent = output(pieces, chunks, True, jnp.bfloat16, ids)
    kept = output(pieces, chunks, False, jnp.float32, ids)
    return (kept + to_sibling(sent).astype(jnp.float32)).astype(jnp.bfloat16)


def solution(mesh):
    return jax.shard_map(
        shards,
        mesh=mesh,
        in_specs=(
            P("slab", "head"),
            P("slab", "head"),
            P("slab", "head"),
            P("slab", "head"),
            P("head"),
            P("head"),
            P("head", "slab"),
            P("slab", None),
            P("slab"),
        ),
        out_specs=P("slab", "head"),
        check_vma=False,
    )
```

```python
import jax
import jax.numpy as jnp
from jax import lax
from jax.experimental import pallas as pl
from jax.experimental.pallas import tpu as pltpu
from jax.sharding import PartitionSpec as P

HD = 128
NX, NZ, NY, NC = 4, 8, 4, 2

norm_eps = 1e-06
masked_score = -1e30
ANY = pl.BlockSpec(memory_space=pl.ANY)
HBM = pl.BlockSpec(memory_space=pltpu.HBM)
SMEM = pl.BlockSpec(memory_space=pltpu.SMEM)
VMEM = pl.BlockSpec(memory_space=pltpu.VMEM)
LARGE = pltpu.CompilerParams(vmem_limit_bytes=16 * 1024 * 1024)
MEDIUM = pltpu.CompilerParams(vmem_limit_bytes=10 * 1024 * 1024)
WHOLE = pltpu.CompilerParams(vmem_limit_bytes=60 * 1024 * 1024)
SMALL = pltpu.CompilerParams(vmem_limit_bytes=4 * 1024 * 1024)
TINY = pltpu.CompilerParams(vmem_limit_bytes=1024 * 1024)
LIGHT = pl.CostEstimate(flops=1, bytes_accessed=1, transcendentals=0)

BLOCKS = (0, 2, 5)
FREE = 4


def group(x):
    return x // 2


def mate(x):
    return x ^ 1


def partner(x):
    return 3 - x


def device(x, z, y, c):
    return ((x * NZ + z) * NY + y) * NC + c


def moved(cells, target):
    pairs = []
    for x in range(NX):
        for z in range(NZ):
            for y in range(NY):
                for c in range(NC):
                    to = target(x, z, y, c)
                    if to is not None:
                        pairs.append((device(x, z, y, c), device(*to)))
    return lax.ppermute(cells, ("slab", "head"), pairs)


def along_x(cells, step):
    return moved(cells, lambda x, z, y, c: ((x + step) % NX, z, y, c))


def along_z(cells, step):
    return moved(cells, lambda x, z, y, c: (x, (z + step) % NZ, y, c))


def along_y(cells, step):
    return moved(cells, lambda x, z, y, c: (x, z, (y + step) % NY, c))


def to_sibling(cells):
    return moved(cells, lambda x, z, y, c: (x, z, y, 1 - c))


def to_partner(cells):
    return moved(cells, lambda x, z, y, c: (partner(x), z, y, c))


def along_slab(cells, step):
    def target(x, z, y, c):
        slab_x = x if c == group(x) else partner(x)
        slab = (slab_x * NZ + z + step) % (NX * NZ)
        to_x = slab // NZ
        chip = to_x if group(to_x) == group(x) else partner(to_x)
        return (chip, slab % NZ, y, group(to_x))

    return moved(cells, target)


def first_shards(shard):
    return moved(
        shard,
        lambda x, z, y, c: (mate(x), z, y, c)
        if c == group(x)
        else (partner(x), z, y, group(x)),
    )


def second_shards(shard):
    return moved(
        shard, lambda x, z, y, c: None if c == group(x) else (x ^ 2, z, y, group(x))
    )


def together(*arrays):
    return lax.optimization_barrier(arrays)


def run(copies):
    for copy in copies:
        copy.start()
    for copy in copies:
        copy.wait()


def join(cells):
    def kernel(*refs):
        out, sems = refs[len(cells) :]
        run([pltpu.make_async_copy(refs[i], out.at[i], sems.at[i]) for i in range(len(cells))])

    return pl.pallas_call(
        kernel,
        out_shape=jax.ShapeDtypeStruct((len(cells),) + cells[0].shape, cells[0].dtype),
        in_specs=[HBM] * len(cells),
        out_specs=VMEM,
        scratch_shapes=[pltpu.SemaphoreType.DMA((len(cells),))],
        compiler_params=WHOLE,
        cost_estimate=LIGHT,
    )(*cells)


def pack(shard, got, got_far, turned, ids):
    kinds = shard.shape[0]

    def kernel(ids_ref, shard_ref, got_ref, far_ref, turned_ref, out, sems):
        free = pltpu.make_async_copy(turned_ref.at[0], out.at[FREE], sems.at[2 * kinds])
        free.start()

        def fill(one, two):
            copies = []
            for w in range(kinds):
                for j, source in enumerate((one, two)):
                    copies.append(
                        pltpu.make_async_copy(
                            source.at[w], out.at[BLOCKS[w] + j], sems.at[2 * w + j]
                        )
                    )
            run(copies)

        @pl.when(ids_ref[4] == 0)
        def _():
            fill(shard_ref, got_ref)

        @pl.when(ids_ref[4] != 0)
        def _():
            fill(got_ref, far_ref)

        free.wait()

    return pl.pallas_call(
        kernel,
        out_shape=jax.ShapeDtypeStruct((2 * kinds + 1,) + shard.shape[1:], shard.dtype),
        in_specs=[SMEM] + [ANY] * 4,
        out_specs=VMEM,
        scratch_shapes=[pltpu.SemaphoreType.DMA((2 * kinds + 1,))],
        compiler_params=SMALL,
        cost_estimate=LIGHT,
    )(ids, shard, got, got_far, turned)


def collect(pieces):
    cells = pieces[0][0]

    def kernel(*refs):
        out, sems = refs[len(pieces) :]
        copies = []
        for i, (_, index) in enumerate(pieces):
            copies.append(pltpu.make_async_copy(refs[i].at[index], out.at[i], sems.at[i]))
        run(copies)

    return pl.pallas_call(
        kernel,
        out_shape=jax.ShapeDtypeStruct((len(pieces),) + cells.shape[-2:], cells.dtype),
        in_specs=[ANY] * len(pieces),
        out_specs=VMEM,
        scratch_shapes=[pltpu.SemaphoreType.DMA((len(pieces),))],
        compiler_params=TINY,
        cost_estimate=LIGHT,
    )(*[piece[0] for piece in pieces])


def arrange(own, swapped, ids):
    tokens, width = own[0].shape
    block = width // 4

    def kernel(ids_ref, *refs):
        sources, swapped_ref, (out, held, sems) = refs[:NY], refs[NY], refs[NY + 1 :]
        copies = []
        for d in range(NY):
            slot = lax.rem(ids_ref[2] + d, NY)
            copies.append(
                pltpu.make_async_copy(sources[d], held.at[slot, ids_ref[3]], sems.at[d])
            )
            copies.append(
                pltpu.make_async_copy(
                    swapped_ref.at[d], held.at[slot, 1 - ids_ref[3]], sems.at[NY + d]
                )
            )
        run(copies)
        x = ids_ref[0]
        mate_x = x + 1 - 2 * lax.rem(x, 2)
        order = [x, mate_x, 3 - x, 3 - mate_x]
        for j in range(NX):
            for core in range(NC):
                for low in range(4):
                    out[4 * core + low, :, j * block : (j + 1) * block] = held[
                        order[j], core, :, low * block : (low + 1) * block
                    ]

    return pl.pallas_call(
        kernel,
        out_shape=jax.ShapeDtypeStruct((NZ, tokens, NX * block), own[0].dtype),
        in_specs=[SMEM] + [ANY] * (NY + 1),
        out_specs=VMEM,
        scratch_shapes=[
            pltpu.VMEM((NY, NC, tokens, width), own[0].dtype),
            pltpu.SemaphoreType.DMA((2 * NY,)),
        ],
        compiler_params=LARGE,
        cost_estimate=LIGHT,
    )(ids, *own, swapped)


def accumulate(total, acts, groups, ids):
    tokens, width = acts.shape[1:]
    rows, feats = groups[0][1][0][1].shape[1:]
    columns = 3 * feats
    chunks = [(i,) + chunk for i, (_, members) in enumerate(groups) for chunk in members]
    slots = len(groups) + sum(len(chunk[3]) for chunk in chunks)
    first = total is None

    def kernel(ids_ref, acts_ref, *refs):
        sources = refs[: len(chunks)]
        rest = refs[len(chunks) :]
        if not first:
            before, rest = rest[0], rest[1:]
        out, weight, held, sems = rest
        copies = [[] for _ in groups]
        used = 0
        for i, (distance, _) in enumerate(groups):
            slot = lax.rem(ids_ref[1] + distance, NZ)
            copies[i].append(pltpu.make_async_copy(acts_ref.at[slot], held.at[i], sems.at[used]))
            used += 1
        for k, (i, opposite, _, parts) in enumerate(chunks):
            kind = 1 - ids_ref[4] if opposite else ids_ref[4]
            for w, begin in parts:
                into = weight.at[i, pl.ds(2 * kind, 2), :, w * feats : (w + 1) * feats]
                copies[i].append(
                    pltpu.make_async_copy(sources[k].at[pl.ds(begin, 2)], into, sems.at[used])
                )
                used += 1
        for members in copies:
            for copy in members:
                copy.start()
        for i in range(len(groups)):
            for copy in copies[i]:
                copy.wait()
            term = jnp.dot(
                held[i],
                weight[i].reshape(NX * rows, columns),
                preferred_element_type=jnp.float32,
            )
            if i:
                out[...] += term
            elif first:
                out[...] = term
            else:
                out[...] = before[...] + term

    return pl.pallas_call(
        kernel,
        out_shape=jax.ShapeDtypeStruct((tokens, columns), jnp.float32),
        in_specs=[SMEM, ANY] + [ANY] * len(chunks) + ([] if first else [VMEM]),
        out_specs=VMEM,
        scratch_shapes=[
            pltpu.VMEM((len(groups), NX, rows, columns), jnp.bfloat16),
            pltpu.VMEM((len(groups), tokens, width), jnp.bfloat16),
            pltpu.SemaphoreType.DMA((slots,)),
        ],
        compiler_params=MEDIUM,
        cost_estimate=LIGHT,
    )(ids, acts, *[chunk[2] for chunk in chunks], *([] if first else [total]))


def assemble(chunks, ids):
    rows, feats = chunks[0][2].shape[1:]
    blocks = [
        (k, i, far, d)
        for k, (far, distances, _) in enumerate(chunks)
        for i, d in enumerate(distances)
        if d is not None
    ]

    def kernel(ids_ref, *refs):
        weights, (out, sems) = refs[: len(chunks)], refs[len(chunks) :]
        copies = []
        for used, (k, i, far, d) in enumerate(blocks):
            z = lax.rem(ids_ref[1] + d, NZ)
            y = lax.rem(ids_ref[0] + far + NY - ids_ref[2], NY)
            into = out.at[z, :, pl.ds(pl.multiple_of(y * feats, HD), feats)]
            copies.append(pltpu.make_async_copy(weights[k].at[i], into, sems.at[used]))
        run(copies)

    return pl.pallas_call(
        kernel,
        out_shape=jax.ShapeDtypeStruct((NZ, rows, NY * feats), chunks[0][2].dtype),
        in_specs=[SMEM] + [ANY] * len(chunks),
        out_specs=VMEM,
        scratch_shapes=[pltpu.SemaphoreType.DMA((len(blocks),))],
        compiler_params=SMALL,
        cost_estimate=LIGHT,
    )(ids, *[chunk[2] for chunk in chunks])


def output(pieces, weight, other, kind, ids):
    tokens, feats = pieces[0][2].shape
    rows = weight.shape[1]

    def kernel(ids_ref, weight_ref, *refs):
        sources, (out, held, sems) = refs[: len(pieces)], refs[len(pieces) :]
        half = 1 - ids_ref[3] if other else ids_ref[3]
        copies = []
        for i, (d, start, cells) in enumerate(pieces):
            slot = lax.rem(ids_ref[2] + d, NY)
            columns = pl.ds(pl.multiple_of(slot * feats, HD), feats)
            into = held.at[pl.ds(start, cells.shape[0]), columns]
            copies.append(pltpu.make_async_copy(sources[i], into, sems.at[i]))
        run(copies)
        out[...] = lax.dot_general(
            held[...],
            weight_ref[pl.ds(4 * half, 4)].reshape(4 * rows, NY * feats),
            (((1,), (1,)), ((), ())),
            preferred_element_type=jnp.float32,
        ).astype(kind)

    return pl.pallas_call(
        kernel,
        out_shape=jax.ShapeDtypeStruct((tokens, 4 * rows), kind),
        in_specs=[SMEM, VMEM] + [ANY] * len(pieces),
        out_specs=VMEM,
        scratch_shapes=[
            pltpu.VMEM((tokens, NY * feats), jnp.bfloat16),
            pltpu.SemaphoreType.DMA((len(pieces),)),
        ],
        compiler_params=MEDIUM,
        cost_estimate=LIGHT,
    )(ids, weight, *[piece[2] for piece in pieces])


def attention(query, sides, factors, local_ids, count):
    tokens, feats = query.shape
    slots = local_ids.shape[0]
    heads = feats // HD

    def kernel(ids_ref, count_ref, q_ref, factor_ref, *refs):
        sources, (out, held, sems) = refs[:3], refs[3:]
        run([pltpu.make_async_copy(sources[i], held.at[i], sems.at[i]) for i in range(3)])
        for h in range(heads):
            q = q_ref[:, h * HD : (h + 1) * HD]
            scores = []
            for s in range(slots):
                key = held[ids_ref[s], :, h * HD : (h + 1) * HD]
                part = lax.dot_general(
                    q, key, (((1,), (1,)), ((), ())), preferred_element_type=jnp.float32
                )
                live = s < count_ref[0]
                scores.append(jnp.where(live, part * factor_ref[ids_ref[s]], masked_score))
            top = scores[0].max(axis=1, keepdims=True)
            for part in scores[1:]:
                top = jnp.maximum(top, part.max(axis=1, keepdims=True))
            weights = [jnp.exp(part - top) for part in scores]
            total = weights[0].sum(axis=1, keepdims=True)
            for part in weights[1:]:
                total = total + part.sum(axis=1, keepdims=True)
            inverse = 1.0 / total
            mixed = None
            for s in range(slots):
                probs = (weights[s] * inverse).astype(jnp.bfloat16)
                value = held[ids_ref[s], :, feats + h * HD : feats + (h + 1) * HD]
                term = jnp.dot(probs, value, preferred_element_type=jnp.float32)
                mixed = term if mixed is None else mixed + term
            out[:, h * HD : (h + 1) * HD] = mixed.astype(jnp.bfloat16)

    return pl.pallas_call(
        kernel,
        out_shape=jax.ShapeDtypeStruct((tokens, feats), jnp.bfloat16),
        in_specs=[SMEM, SMEM, VMEM, VMEM] + [ANY] * 3,
        out_specs=VMEM,
        scratch_shapes=[
            pltpu.VMEM((3, tokens, 2 * feats), jnp.bfloat16),
            pltpu.SemaphoreType.DMA((3,)),
        ],
        compiler_params=LARGE,
        cost_estimate=LIGHT,
    )(local_ids, count, query, factors, *sides)


def shards(
    activations, w_query, w_key, w_value, query_gain, key_gain, w_output, kv_tiles, kv_count
):
    slab = lax.axis_index("slab")
    head = lax.axis_index("head")
    x, z, y, c = slab // NZ, slab % NZ, head // NC, head % NC
    home = c == x // 2
    kind = jnp.where(home, 0, 1)
    ids = jnp.stack([x, z, y, c, kind]).astype(jnp.int32)
    feats = w_query.shape[1]
    features = feats * NY * NC

    whole = tuple(enumerate(BLOCKS))
    half = activations.shape[0] // 2

    def pair_of_chunks(cells, swapped, parts):
        return [(False, cells, parts), (True, swapped, parts)]

    def groups_of(step, ahead, behind, ahead_swapped, behind_swapped):
        return [
            (step, pair_of_chunks(ahead, ahead_swapped, whole)),
            (NZ - step, pair_of_chunks(behind, behind_swapped, whole)),
        ]

    shard = join([w_query, w_key, w_value])
    turned = moved(w_output.T, lambda x, z, y, c: ((x + y) % NX, z, x, 1 - c))
    got, got_far, own_1, own_3, turned = together(
        first_shards(shard),
        second_shards(shard),
        along_y(activations, -1),
        along_y(activations, 1),
        to_sibling(collect([(turned[None], 0)] + [(shard, i) for i in range(3)])),
    )
    mine = pack(shard, got, got_far, turned, ids)

    mine, own_0, own_1, own_3 = together(mine, activations, own_1, own_3)
    ahead_1, behind_1, own_2a, own_2b, pair_0 = together(
        along_z(mine, -1),
        along_z(mine, 1),
        along_y(own_1[:half], -1),
        along_y(own_3[half:], 1),
        to_partner(own_0),
    )

    own_2 = jnp.concatenate([own_2a, own_2b])
    pair_1, pair_3 = along_y(pair_0, -1), along_y(pair_0, 1)
    early = together(mine, ahead_1, behind_1, pair_1, pair_3)
    ahead_2, behind_2, pair_1, pair_3, pair_2, mine_s, ahead_1s, behind_1s = together(
        along_z(ahead_1, -1),
        along_z(behind_1, 1),
        pair_1,
        pair_3,
        to_partner(own_2),
        to_sibling(early[0]),
        to_sibling(early[1]),
        to_sibling(early[2]),
    )

    owns = (own_0, own_1, own_2, own_3)
    pairs = (pair_0, pair_1, pair_2, pair_3)
    kept = [jnp.where(home, own, pair) for own, pair in zip(owns, pairs)]
    sent = jnp.stack([jnp.where(home, pair, own) for own, pair in zip(owns, pairs)])
    swapped = to_sibling(sent)
    acts = arrange(kept, swapped, ids)
    total = accumulate(None, acts, [(0, pair_of_chunks(mine, mine_s, whole))], ids)
    total = accumulate(total, acts, groups_of(1, ahead_1, behind_1, ahead_1s, behind_1s), ids)
    late = together(ahead_2, behind_2, swapped)
    ahead_2s, behind_2s = to_sibling(late[0]), to_sibling(late[1])
    small = jnp.concatenate(
        [query_gain, key_gain, kv_tiles[0].astype(jnp.float32), kv_count.astype(jnp.float32)]
    )
    out_first = collect([(cells, FREE) for cells in (mine, ahead_1, behind_1)])
    small_here, out_first = together(small, out_first, ahead_2s, behind_2s)[:2]
    ahead_3, behind_3, ahead_2s, behind_2s, out_ahead, out_behind, small_got, total = together(
        along_z(ahead_2, -1),
        along_z(behind_2, 1),
        ahead_2s,
        behind_2s,
        along_x(out_first, -1),
        along_x(out_first, 1),
        moved(small_here, lambda x, z, y, c: (partner(x), z, y, 1 - c)),
        total,
    )
    small = jnp.where(home, small, small_got)
    gains = small[: 2 * feats].reshape(2, feats)
    lists = small[2 * feats :].astype(jnp.int32)
    slab_here = jnp.where(home, x, 3 - x) * NZ + z

    ahead_3s, behind_3s = to_sibling(ahead_3), to_sibling(behind_3)
    total = accumulate(total, acts, groups_of(2, ahead_2, behind_2, ahead_2s, behind_2s), ids)
    ahead_4, behind_4 = along_z(ahead_3[:FREE], -1), along_z(behind_3[FREE:], 1)
    blocks = [(cells, FREE) for cells in (ahead_2, behind_2, ahead_3, behind_3)]
    up_1 = collect([(out_ahead, 0), (out_ahead, 1)] + blocks)
    down_1 = collect([(out_behind, 2)] + blocks)
    up_1, down_1 = together(up_1, down_1, ahead_3s, behind_3s)[:2]
    late_ahead, late_behind, total = together(ahead_4, behind_4, total)
    total = accumulate(total, acts, groups_of(3, ahead_3, behind_3, ahead_3s, behind_3s), ids)
    ahead_4, behind_4, ahead_4s, behind_4s, up_got, down_got, total = together(
        ahead_4,
        behind_4,
        to_sibling(late_ahead),
        to_sibling(late_behind),
        along_x(up_1, -1),
        along_x(down_1, 1),
        total,
    )
    members = pair_of_chunks(ahead_4, ahead_4s, whole[:2])
    members += pair_of_chunks(behind_4, behind_4s, ((2, 1),))
    total = accumulate(total, acts, [(4, members)], ids)

    q_raw, k_raw, v_raw = total[:, :feats], total[:, feats : 2 * feats], total[:, 2 * feats :]
    sums = jnp.stack([jnp.sum(q_raw * q_raw, axis=1), jnp.sum(k_raw * k_raw, axis=1)])
    sides = jnp.concatenate([k_raw * gains[1], v_raw], axis=1).astype(jnp.bfloat16)
    sums, sides = together(sums, sides)
    side_before, side_next = along_slab(sides, 1), along_slab(sides, -1)
    sums = sums + moved(sums, lambda x, z, y, c: (x, z, y ^ 1, c))
    sums = sums + moved(sums, lambda x, z, y, c: (x, z, y ^ 2, c))
    sums = sums + to_partner(sums)
    norms = lax.rsqrt(sums / features + norm_eps)
    query = (q_raw * norms[0][:, None] * gains[0]).astype(jnp.bfloat16)
    factor = norms[1] * HD ** (-0.5)
    out_last = behind_4[:1]
    up_2 = collect([(up_got, 2), (up_got, 3), (out_last, 0)])
    down_2 = collect([(down_got, 3), (down_got, 4), (out_last, 0)])
    up_2, down_2, out_last = together(up_2, down_2, out_last, sums)[:3]
    up_far, down_far, out_far = along_x(up_2, -1), along_x(down_2, 1), along_x(out_last, 2)
    first, second = (0, 1, 7), (2, 6, 3, 5)
    chunks = [(0, first, out_first), (1, first, out_ahead), (3, first, out_behind)]
    chunks += [(2, first[:2] + (None,) * 4, up_got), (2, first[2:] + (None,) * 4, down_got)]
    chunks += [(0, (None,) * 2 + second, up_1), (1, (None,) * 2 + second, up_got)]
    chunks += [(3, (None,) + second, down_got)]
    chunks += [(2, second[:2] + (None,), up_far), (2, second[2:] + (None,), down_far)]
    chunks += [(0, (None, None, 4), up_2), (1, (None, None, 4), up_far)]
    chunks += [(3, (None, None, 4), down_far), (2, (4,), out_far)]
    factor, side_before, side_next = together(factor, side_before, side_next)
    factor_before, factor_next = together(along_slab(factor, 1), along_slab(factor, -1))
    factors = jnp.stack([factor_before, factor, factor_next])[:, None, :]
    local_ids = jnp.clip(lists[:3] - slab_here + 1, 0, 2).astype(jnp.int32)
    attended = attention(
        query,
        (side_before, sides, side_next),
        factors,
        local_ids,
        lists[3:],
    )

    pieces = [None] * NY
    for d in (0, 1, 3):

        def target(x, z, y, c, d=d):
            if c == group(x):
                return (x, z, (y + d) % NY, c) if d else None
            return (partner(x), z, (y + d) % NY, group(x))

        pieces[-d % NY] = moved(attended, target)
    near, up, down = together(pieces[0], pieces[1], pieces[3])
    far_1, far_2 = along_y(up[:half], -1), along_y(down[half:], 1)
    near = jnp.where(home, attended, near)
    far_1, far_2, weight = together(far_1, far_2, assemble(chunks, ids))
    pieces = [(0, 0, near), (1, 0, up), (3, 0, down), (2, 0, far_1), (2, half, far_2)]
    sent = output(pieces, weight, True, jnp.bfloat16, ids)
    kept = output(pieces, weight, False, jnp.float32, ids)
    return (kept + to_sibling(sent).astype(jnp.float32)).astype(jnp.bfloat16)


def solution(mesh):
    return jax.shard_map(
        shards,
        mesh=mesh,
        in_specs=(
            P("slab", "head"),
            P("slab", "head"),
            P("slab", "head"),
            P("slab", "head"),
            P("head"),
            P("head"),
            P("head", "slab"),
            P("slab", None),
            P("slab"),
        ),
        out_specs=P("slab", "head"),
        check_vma=False,
    )
```

```python
import jax
import jax.numpy as jnp
from jax import lax
from jax.experimental import pallas as pl
from jax.experimental.pallas import tpu as pltpu
from jax.sharding import PartitionSpec as P

HD = 128
NX, NZ, NY, NC = 4, 8, 4, 2

norm_eps = 1e-06
masked_score = -1e30
ANY = pl.BlockSpec(memory_space=pl.ANY)
HBM = pl.BlockSpec(memory_space=pltpu.HBM)
SMEM = pl.BlockSpec(memory_space=pltpu.SMEM)
VMEM = pl.BlockSpec(memory_space=pltpu.VMEM)
LARGE = pltpu.CompilerParams(vmem_limit_bytes=16 * 1024 * 1024)
MEDIUM = pltpu.CompilerParams(vmem_limit_bytes=10 * 1024 * 1024)
WHOLE = pltpu.CompilerParams(vmem_limit_bytes=60 * 1024 * 1024)
SMALL = pltpu.CompilerParams(vmem_limit_bytes=4 * 1024 * 1024)
TINY = pltpu.CompilerParams(vmem_limit_bytes=1024 * 1024)
LIGHT = pl.CostEstimate(flops=1, bytes_accessed=1, transcendentals=0)

BLOCKS = (0, 2, 5)
FREE = 4


def group(x):
    return x // 2


def mate(x):
    return x ^ 1


def partner(x):
    return 3 - x


def device(x, z, y, c):
    return ((x * NZ + z) * NY + y) * NC + c


def moved(cells, target):
    pairs = []
    for x in range(NX):
        for z in range(NZ):
            for y in range(NY):
                for c in range(NC):
                    to = target(x, z, y, c)
                    if to is not None:
                        pairs.append((device(x, z, y, c), device(*to)))
    return lax.ppermute(cells, ("slab", "head"), pairs)


def along_x(cells, step):
    return moved(cells, lambda x, z, y, c: ((x + step) % NX, z, y, c))


def along_z(cells, step):
    return moved(cells, lambda x, z, y, c: (x, (z + step) % NZ, y, c))


def along_y(cells, step):
    return moved(cells, lambda x, z, y, c: (x, z, (y + step) % NY, c))


def to_sibling(cells):
    return moved(cells, lambda x, z, y, c: (x, z, y, 1 - c))


def to_partner(cells):
    return moved(cells, lambda x, z, y, c: (partner(x), z, y, c))


def along_slab(cells, step):
    def target(x, z, y, c):
        slab_x = x if c == group(x) else partner(x)
        slab = (slab_x * NZ + z + step) % (NX * NZ)
        to_x = slab // NZ
        chip = to_x if group(to_x) == group(x) else partner(to_x)
        return (chip, slab % NZ, y, group(to_x))

    return moved(cells, target)


def first_shards(shard):
    return moved(
        shard,
        lambda x, z, y, c: (mate(x), z, y, c)
        if c == group(x)
        else (partner(x), z, y, group(x)),
    )


def second_shards(shard):
    return moved(
        shard, lambda x, z, y, c: None if c == group(x) else (x ^ 2, z, y, group(x))
    )


def together(*arrays):
    return lax.optimization_barrier(arrays)


def run(copies):
    for copy in copies:
        copy.start()
    for copy in copies:
        copy.wait()


def join(cells):
    def kernel(*refs):
        out, sems = refs[len(cells) :]
        run([pltpu.make_async_copy(refs[i], out.at[i], sems.at[i]) for i in range(len(cells))])

    return pl.pallas_call(
        kernel,
        out_shape=jax.ShapeDtypeStruct((len(cells),) + cells[0].shape, cells[0].dtype),
        in_specs=[HBM] * len(cells),
        out_specs=VMEM,
        scratch_shapes=[pltpu.SemaphoreType.DMA((len(cells),))],
        compiler_params=WHOLE,
        cost_estimate=LIGHT,
    )(*cells)


def pack(shard, got, got_far, turned, ids):
    kinds = shard.shape[0]

    def kernel(ids_ref, shard_ref, got_ref, far_ref, turned_ref, out, sems):
        free = pltpu.make_async_copy(turned_ref.at[0], out.at[FREE], sems.at[2 * kinds])
        free.start()

        def fill(one, two):
            copies = []
            for w in range(kinds):
                for j, source in enumerate((one, two)):
                    copies.append(
                        pltpu.make_async_copy(
                            source.at[w], out.at[BLOCKS[w] + j], sems.at[2 * w + j]
                        )
                    )
            run(copies)

        @pl.when(ids_ref[4] == 0)
        def _():
            fill(shard_ref, got_ref)

        @pl.when(ids_ref[4] != 0)
        def _():
            fill(got_ref, far_ref)

        free.wait()

    return pl.pallas_call(
        kernel,
        out_shape=jax.ShapeDtypeStruct((2 * kinds + 1,) + shard.shape[1:], shard.dtype),
        in_specs=[SMEM] + [ANY] * 4,
        out_specs=VMEM,
        scratch_shapes=[pltpu.SemaphoreType.DMA((2 * kinds + 1,))],
        compiler_params=SMALL,
        cost_estimate=LIGHT,
    )(ids, shard, got, got_far, turned)


def collect(pieces):
    cells = pieces[0][0]

    def kernel(*refs):
        out, sems = refs[len(pieces) :]
        copies = []
        for i, (_, index) in enumerate(pieces):
            copies.append(pltpu.make_async_copy(refs[i].at[index], out.at[i], sems.at[i]))
        run(copies)

    return pl.pallas_call(
        kernel,
        out_shape=jax.ShapeDtypeStruct((len(pieces),) + cells.shape[-2:], cells.dtype),
        in_specs=[ANY] * len(pieces),
        out_specs=VMEM,
        scratch_shapes=[pltpu.SemaphoreType.DMA((len(pieces),))],
        compiler_params=TINY,
        cost_estimate=LIGHT,
    )(*[piece[0] for piece in pieces])


def arrange(own, swapped, ids):
    tokens, width = own[0].shape
    block = width // 4

    def kernel(ids_ref, *refs):
        sources, swapped_ref, (out, held, sems) = refs[:NY], refs[NY], refs[NY + 1 :]
        copies = []
        for d in range(NY):
            slot = lax.rem(ids_ref[2] + d, NY)
            copies.append(
                pltpu.make_async_copy(sources[d], held.at[slot, ids_ref[3]], sems.at[d])
            )
            copies.append(
                pltpu.make_async_copy(
                    swapped_ref.at[d], held.at[slot, 1 - ids_ref[3]], sems.at[NY + d]
                )
            )
        run(copies)
        x = ids_ref[0]
        mate_x = x + 1 - 2 * lax.rem(x, 2)
        order = [x, mate_x, 3 - x, 3 - mate_x]
        for j in range(NX):
            for core in range(NC):
                for low in range(4):
                    out[4 * core + low, :, j * block : (j + 1) * block] = held[
                        order[j], core, :, low * block : (low + 1) * block
                    ]

    return pl.pallas_call(
        kernel,
        out_shape=jax.ShapeDtypeStruct((NZ, tokens, NX * block), own[0].dtype),
        in_specs=[SMEM] + [ANY] * (NY + 1),
        out_specs=VMEM,
        scratch_shapes=[
            pltpu.VMEM((NY, NC, tokens, width), own[0].dtype),
            pltpu.SemaphoreType.DMA((2 * NY,)),
        ],
        compiler_params=LARGE,
        cost_estimate=LIGHT,
    )(ids, *own, swapped)


def accumulate(total, acts, groups, ids):
    tokens, width = acts.shape[1:]
    rows, feats = groups[0][1][0][1].shape[1:]
    columns = 3 * feats
    chunks = [(i,) + chunk for i, (_, members) in enumerate(groups) for chunk in members]
    slots = len(groups) + sum(len(chunk[3]) for chunk in chunks)
    first = total is None

    def kernel(ids_ref, acts_ref, *refs):
        sources = refs[: len(chunks)]
        rest = refs[len(chunks) :]
        if not first:
            before, rest = rest[0], rest[1:]
        out, weight, held, sems = rest
        copies = [[] for _ in groups]
        used = 0
        for i, (distance, _) in enumerate(groups):
            slot = lax.rem(ids_ref[1] + distance, NZ)
            copies[i].append(pltpu.make_async_copy(acts_ref.at[slot], held.at[i], sems.at[used]))
            used += 1
        for k, (i, opposite, _, parts) in enumerate(chunks):
            kind = 1 - ids_ref[4] if opposite else ids_ref[4]
            for w, begin in parts:
                into = weight.at[i, pl.ds(2 * kind, 2), :, w * feats : (w + 1) * feats]
                copies[i].append(
                    pltpu.make_async_copy(sources[k].at[pl.ds(begin, 2)], into, sems.at[used])
                )
                used += 1
        for members in copies:
            for copy in members:
                copy.start()
        for i in range(len(groups)):
            for copy in copies[i]:
                copy.wait()
            term = jnp.dot(
                held[i],
                weight[i].reshape(NX * rows, columns),
                preferred_element_type=jnp.float32,
            )
            if i:
                out[...] += term
            elif first:
                out[...] = term
            else:
                out[...] = before[...] + term

    return pl.pallas_call(
        kernel,
        out_shape=jax.ShapeDtypeStruct((tokens, columns), jnp.float32),
        in_specs=[SMEM, ANY] + [ANY] * len(chunks) + ([] if first else [VMEM]),
        out_specs=VMEM,
        scratch_shapes=[
            pltpu.VMEM((len(groups), NX, rows, columns), jnp.bfloat16),
            pltpu.VMEM((len(groups), tokens, width), jnp.bfloat16),
            pltpu.SemaphoreType.DMA((slots,)),
        ],
        compiler_params=MEDIUM,
        cost_estimate=LIGHT,
    )(ids, acts, *[chunk[2] for chunk in chunks], *([] if first else [total]))


def assemble(chunks, ids):
    rows, feats = chunks[0][2].shape[1:]
    blocks = [
        (k, i, far, d)
        for k, (far, distances, _) in enumerate(chunks)
        for i, d in enumerate(distances)
        if d is not None
    ]

    def kernel(ids_ref, *refs):
        weights, (out, sems) = refs[: len(chunks)], refs[len(chunks) :]
        copies = []
        for used, (k, i, far, d) in enumerate(blocks):
            z = lax.rem(ids_ref[1] + d, NZ)
            y = lax.rem(ids_ref[0] + far + NY - ids_ref[2], NY)
            into = out.at[z, :, pl.ds(pl.multiple_of(y * feats, HD), feats)]
            copies.append(pltpu.make_async_copy(weights[k].at[i], into, sems.at[used]))
        run(copies)

    return pl.pallas_call(
        kernel,
        out_shape=jax.ShapeDtypeStruct((NZ, rows, NY * feats), chunks[0][2].dtype),
        in_specs=[SMEM] + [ANY] * len(chunks),
        out_specs=VMEM,
        scratch_shapes=[pltpu.SemaphoreType.DMA((len(blocks),))],
        compiler_params=SMALL,
        cost_estimate=LIGHT,
    )(ids, *[chunk[2] for chunk in chunks])


def output(pieces, weight, other, kind, ids):
    tokens, feats = pieces[0][2].shape
    rows = weight.shape[1]

    def kernel(ids_ref, weight_ref, *refs):
        sources, (out, held, sems) = refs[: len(pieces)], refs[len(pieces) :]
        half = 1 - ids_ref[3] if other else ids_ref[3]
        copies = []
        for i, (d, start, cells) in enumerate(pieces):
            slot = lax.rem(ids_ref[2] + d, NY)
            columns = pl.ds(pl.multiple_of(slot * feats, HD), feats)
            into = held.at[pl.ds(start, cells.shape[0]), columns]
            copies.append(pltpu.make_async_copy(sources[i], into, sems.at[i]))
        run(copies)
        out[...] = lax.dot_general(
            held[...],
            weight_ref[pl.ds(4 * half, 4)].reshape(4 * rows, NY * feats),
            (((1,), (1,)), ((), ())),
            preferred_element_type=jnp.float32,
        ).astype(kind)

    return pl.pallas_call(
        kernel,
        out_shape=jax.ShapeDtypeStruct((tokens, 4 * rows), kind),
        in_specs=[SMEM, VMEM] + [ANY] * len(pieces),
        out_specs=VMEM,
        scratch_shapes=[
            pltpu.VMEM((tokens, NY * feats), jnp.bfloat16),
            pltpu.SemaphoreType.DMA((len(pieces),)),
        ],
        compiler_params=MEDIUM,
        cost_estimate=LIGHT,
    )(ids, weight, *[piece[2] for piece in pieces])


def attention(query, sides, factors, local_ids, count):
    tokens, feats = query.shape
    slots = local_ids.shape[0]
    heads = feats // HD

    def kernel(ids_ref, count_ref, q_ref, factor_ref, *refs):
        sources, (out, held, sems) = refs[:3], refs[3:]
        run([pltpu.make_async_copy(sources[i], held.at[i], sems.at[i]) for i in range(3)])
        for h in range(heads):
            q = q_ref[:, h * HD : (h + 1) * HD]
            scores = []
            for s in range(slots):
                key = held[ids_ref[s], :, h * HD : (h + 1) * HD]
                part = lax.dot_general(
                    q, key, (((1,), (1,)), ((), ())), preferred_element_type=jnp.float32
                )
                live = s < count_ref[0]
                scores.append(jnp.where(live, part * factor_ref[ids_ref[s]], masked_score))
            top = scores[0].max(axis=1, keepdims=True)
            for part in scores[1:]:
                top = jnp.maximum(top, part.max(axis=1, keepdims=True))
            weights = [jnp.exp(part - top) for part in scores]
            total = weights[0].sum(axis=1, keepdims=True)
            for part in weights[1:]:
                total = total + part.sum(axis=1, keepdims=True)
            inverse = 1.0 / total
            mixed = None
            for s in range(slots):
                probs = (weights[s] * inverse).astype(jnp.bfloat16)
                value = held[ids_ref[s], :, feats + h * HD : feats + (h + 1) * HD]
                term = jnp.dot(probs, value, preferred_element_type=jnp.float32)
                mixed = term if mixed is None else mixed + term
            out[:, h * HD : (h + 1) * HD] = mixed.astype(jnp.bfloat16)

    return pl.pallas_call(
        kernel,
        out_shape=jax.ShapeDtypeStruct((tokens, feats), jnp.bfloat16),
        in_specs=[SMEM, SMEM, VMEM, VMEM] + [ANY] * 3,
        out_specs=VMEM,
        scratch_shapes=[
            pltpu.VMEM((3, tokens, 2 * feats), jnp.bfloat16),
            pltpu.SemaphoreType.DMA((3,)),
        ],
        compiler_params=LARGE,
        cost_estimate=LIGHT,
    )(local_ids, count, query, factors, *sides)


def shards(
    activations, w_query, w_key, w_value, query_gain, key_gain, w_output, kv_tiles, kv_count
):
    slab = lax.axis_index("slab")
    head = lax.axis_index("head")
    x, z, y, c = slab // NZ, slab % NZ, head // NC, head % NC
    home = c == x // 2
    kind = jnp.where(home, 0, 1)
    ids = jnp.stack([x, z, y, c, kind]).astype(jnp.int32)
    feats = w_query.shape[1]
    features = feats * NY * NC

    whole = tuple(enumerate(BLOCKS))
    half = activations.shape[0] // 2

    def pair_of_chunks(cells, swapped, parts):
        return [(False, cells, parts), (True, swapped, parts)]

    def groups_of(step, ahead, behind, ahead_swapped, behind_swapped):
        return [
            (step, pair_of_chunks(ahead, ahead_swapped, whole)),
            (NZ - step, pair_of_chunks(behind, behind_swapped, whole)),
        ]

    shard = join([w_query, w_key, w_value])
    turned = moved(w_output.T, lambda x, z, y, c: ((x + y) % NX, z, x, 1 - c))
    got, got_far, own_1, own_3, turned = together(
        first_shards(shard),
        second_shards(shard),
        along_y(activations, -1),
        along_y(activations, 1),
        to_sibling(collect([(turned[None], 0)] + [(shard, i) for i in range(3)])),
    )
    mine = pack(shard, got, got_far, turned, ids)

    mine, own_0, own_1, own_3 = together(mine, activations, own_1, own_3)
    ahead_1, behind_1, own_2a, own_2b, pair_0 = together(
        along_z(mine, -1),
        along_z(mine, 1),
        along_y(own_1[:half], -1),
        along_y(own_3[half:], 1),
        to_partner(own_0),
    )

    own_2 = jnp.concatenate([own_2a, own_2b])
    pair_1, pair_3 = along_y(pair_0, -1), along_y(pair_0, 1)
    early = together(mine, ahead_1, behind_1, pair_1, pair_3)
    ahead_2, behind_2, pair_1, pair_3, pair_2, mine_s, ahead_1s, behind_1s = together(
        along_z(ahead_1, -1),
        along_z(behind_1, 1),
        pair_1,
        pair_3,
        to_partner(own_2),
        to_sibling(early[0]),
        to_sibling(early[1]),
        to_sibling(early[2]),
    )

    owns = (own_0, own_1, own_2, own_3)
    pairs = (pair_0, pair_1, pair_2, pair_3)
    kept = [jnp.where(home, own, pair) for own, pair in zip(owns, pairs)]
    sent = jnp.stack([jnp.where(home, pair, own) for own, pair in zip(owns, pairs)])
    swapped = to_sibling(sent)
    acts = arrange(kept, swapped, ids)
    total = accumulate(None, acts, [(0, pair_of_chunks(mine, mine_s, whole))], ids)
    total = accumulate(total, acts, groups_of(1, ahead_1, behind_1, ahead_1s, behind_1s), ids)
    late = together(ahead_2, behind_2, swapped)
    ahead_2s, behind_2s = to_sibling(late[0]), to_sibling(late[1])
    small = jnp.concatenate(
        [query_gain, key_gain, kv_tiles[0].astype(jnp.float32), kv_count.astype(jnp.float32)]
    )
    out_first = collect([(cells, FREE) for cells in (mine, ahead_1, behind_1, ahead_2)])
    small_here, out_first = together(small, out_first, ahead_2s, behind_2s)[:2]
    ahead_3, behind_3, ahead_2s, behind_2s, out_ahead, out_behind, small_got, total = together(
        along_z(ahead_2, -1),
        along_z(behind_2, 1),
        ahead_2s,
        behind_2s,
        along_x(out_first, -1),
        along_x(out_first, 1),
        moved(small_here, lambda x, z, y, c: (partner(x), z, y, 1 - c)),
        total,
    )
    small = jnp.where(home, small, small_got)
    gains = small[: 2 * feats].reshape(2, feats)
    lists = small[2 * feats :].astype(jnp.int32)
    slab_here = jnp.where(home, x, 3 - x) * NZ + z

    ahead_3s, behind_3s = to_sibling(ahead_3), to_sibling(behind_3)
    total = accumulate(total, acts, groups_of(2, ahead_2, behind_2, ahead_2s, behind_2s), ids)
    ahead_4, behind_4 = along_z(ahead_3[:FREE], -1), along_z(behind_3[FREE:], 1)
    blocks = [(cells, FREE) for cells in (behind_2, ahead_3, behind_3)]
    up_1 = collect([(out_ahead, 0), (out_ahead, 1)] + blocks)
    down_1 = collect([(out_behind, 2), (out_behind, 3)] + blocks)
    up_1, down_1 = together(up_1, down_1, ahead_3s, behind_3s)[:2]
    late_ahead, late_behind, total = together(ahead_4, behind_4, total)
    total = accumulate(total, acts, groups_of(3, ahead_3, behind_3, ahead_3s, behind_3s), ids)
    ahead_4, behind_4, ahead_4s, behind_4s, up_got, down_got, total = together(
        ahead_4,
        behind_4,
        to_sibling(late_ahead),
        to_sibling(late_behind),
        along_x(up_1, -1),
        along_x(down_1, 1),
        total,
    )
    members = pair_of_chunks(ahead_4, ahead_4s, whole[:2])
    members += pair_of_chunks(behind_4, behind_4s, ((2, 1),))
    total = accumulate(total, acts, [(4, members)], ids)

    q_raw, k_raw = total[:, :feats], total[:, feats : 2 * feats]
    scales = jnp.concatenate([gains[1], jnp.ones_like(gains[1])])
    sums = jnp.stack([jnp.sum(q_raw * q_raw, axis=1), jnp.sum(k_raw * k_raw, axis=1)])
    sides = (total[:, feats:] * scales).astype(jnp.bfloat16)
    sums, sides = together(sums, sides)
    side_before, side_next = along_slab(sides, 1), along_slab(sides, -1)
    sums = sums + moved(sums, lambda x, z, y, c: (x, z, y ^ 1, c))
    sums = sums + moved(sums, lambda x, z, y, c: (x, z, y ^ 2, c))
    sums = sums + to_partner(sums)
    norms = lax.rsqrt(sums / features + norm_eps)
    query = (q_raw * norms[0][:, None] * gains[0]).astype(jnp.bfloat16)
    factor = norms[1] * HD ** (-0.5)
    out_last = behind_4[:1]
    up_2 = collect([(up_got, 2), (up_got, 3), (out_last, 0)])
    down_2 = collect([(down_got, 4), (out_last, 0)])
    up_2, down_2, out_last = together(up_2, down_2, out_last, sums)[:3]
    up_far, down_far, out_far = along_x(up_2, -1), along_x(down_2, 1), along_x(out_last, 2)
    first, second = (0, 1, 7, 2), (6, 3, 5)
    chunks = [(0, first, out_first), (1, first, out_ahead), (3, first, out_behind)]
    chunks += [(2, first[:2] + (None,) * 3, up_got), (2, first[2:] + (None,) * 3, down_got)]
    chunks += [(0, (None,) * 2 + second, up_1), (1, (None,) * 2 + second, up_got)]
    chunks += [(3, (None,) * 2 + second, down_got)]
    chunks += [(2, second[:2] + (None,), up_far), (2, second[2:] + (None,), down_far)]
    chunks += [(0, (None, None, 4), up_2), (1, (None, None, 4), up_far)]
    chunks += [(3, (None, 4), down_far), (2, (4,), out_far)]
    factor, side_before, side_next = together(factor, side_before, side_next)
    factor_before, factor_next = together(along_slab(factor, 1), along_slab(factor, -1))
    factors = jnp.stack([factor_before, factor, factor_next])[:, None, :]
    local_ids = jnp.clip(lists[:3] - slab_here + 1, 0, 2).astype(jnp.int32)
    attended = attention(
        query,
        (side_before, sides, side_next),
        factors,
        local_ids,
        lists[3:],
    )

    pieces = [None] * NY
    for d in (0, 1, 3):

        def target(x, z, y, c, d=d):
            if c == group(x):
                return (x, z, (y + d) % NY, c) if d else None
            return (partner(x), z, (y + d) % NY, group(x))

        pieces[-d % NY] = moved(attended, target)
    near, up, down = together(pieces[0], pieces[1], pieces[3])
    far_1, far_2 = along_y(up[:half], -1), along_y(down[half:], 1)
    near = jnp.where(home, attended, near)
    far_1, far_2, weight = together(far_1, far_2, assemble(chunks, ids))
    pieces = [(0, 0, near), (1, 0, up), (3, 0, down), (2, 0, far_1), (2, half, far_2)]
    sent = output(pieces, weight, True, jnp.bfloat16, ids)
    kept = output(pieces, weight, False, jnp.float32, ids)
    return (kept + to_sibling(sent).astype(jnp.float32)).astype(jnp.bfloat16)


def solution(mesh):
    return jax.shard_map(
        shards,
        mesh=mesh,
        in_specs=(
            P("slab", "head"),
            P("slab", "head"),
            P("slab", "head"),
            P("slab", "head"),
            P("head"),
            P("head"),
            P("head", "slab"),
            P("slab", None),
            P("slab"),
        ),
        out_specs=P("slab", "head"),
        check_vma=False,
    )
```
